256 devices in a mesh: seq: 64 (over y, z, x_hi), mp: 4 (over x_lo, core).
Axes of the slice: x: 4 (x_hi: 2, x_lo: 2; x = x_hi * 2 + x_lo), y: 4, z: 8, core: 2. Of those that a mesh axis runs over, the one named last changes fastest.
Arguments:
- queries: bfloat16 [32768, 2048], P('seq', 'mp'), may hold values from -5 to 5
- key_rows: bfloat16 [32768, 2048], P('seq', 'mp'), may hold values from -5 to 5
- value_rows: bfloat16 [32768, 2048], P('seq', 'mp'), may hold values from -6 to 6
- out_weight: bfloat16 [2048, 2048], P('mp'), may hold values from -3 to 3
- grad_out: bfloat16 [32768, 2048], P('seq', 'mp'), may hold values from -1.5 to 1.5
- offsets: int32 [2, 16], P(None, 'mp'), may hold values from 0 to 63, as said below
Outputs:
- mixed: bfloat16 [32768, 2048], P('seq', 'mp')
- query_grad: bfloat16 [32768, 2048], P('seq', 'mp')
- key_grad: bfloat16 [32768, 2048], P('seq', 'mp')
- value_grad: bfloat16 [32768, 2048], P('seq', 'mp')
The draws below stay inside these ranges and needn't reach their ends.
Inputs may be any that keep to these rules, and one draw needn't show every extreme that they name: offsets[0, h] lies in 0 to 3 and offsets[1, h] in 0 to 63; in each row some head has the largest value and another head has 0.
All inputs are finite; a program needn't handle non-finite values.
Results may differ from the reference program's by a relative error of at most 0.024.
Values may be sent and summed in bfloat16 or wider, within the bound.
A program may use at most 128 MiB of HBM per device.

```python
import jax
import jax.numpy as jnp
from jax import lax

D = 2048
HEADS = 16
HEAD_DIM = 128
TOK_DEV = 512
GROUP = 4
TOKENS = 32768
N_SEQ = 64


def aligned_rows(key):
    base_query = jnp.clip(jax.random.normal(jax.random.fold_in(key, 11), (TOKENS, D), jnp.float32), -5.0, 5.0)
    base_key = jnp.clip(jax.random.normal(jax.random.fold_in(key, 12), (TOKENS, D), jnp.float32), -5.0, 5.0)
    row_index = jnp.arange(TOKENS)[:, None]
    slot_index = row_index % 64
    queries = base_query
    keys_out = base_key
    share = 3.0 / HEAD_DIM ** 0.5
    echo = jnp.roll(queries, -(TOKENS // 2), 0)
    keys_out = jnp.clip(keys_out + jnp.where(slot_index < 61, share * echo, 0.0), -5.0, 5.0)
    return (queries, keys_out)


def draw_queries(key, part):
    drawn = aligned_rows(key)
    return drawn[0].astype(jnp.bfloat16)


def draw_key_rows(key, part):
    drawn = aligned_rows(key)
    return drawn[1].astype(jnp.bfloat16)


def draw_offsets(key, part):
    key = jax.random.fold_in(key, 7)
    near_shift = jax.random.randint(jax.random.fold_in(key, 1), (HEADS,), 0, GROUP)
    far_shift = jax.random.randint(jax.random.fold_in(key, 2), (HEADS,), 0, N_SEQ)
    chosen = jax.random.randint(jax.random.fold_in(key, 3), (), 0, HEADS)
    second = (chosen + 1) % HEADS
    near_shift = near_shift.at[chosen].set(GROUP - 1).at[second].set(0)
    far_shift = far_shift.at[chosen].set(N_SEQ - 1).at[second].set(0)
    return jnp.stack([near_shift, far_shift]).astype(jnp.int32)


def steps_of(key, extent, cuts, low, high):
    level = 1.0
    for dim, shards_of in cuts:
        draws = jax.random.uniform(jax.random.fold_in(jax.random.fold_in(key, 6), dim), (shards_of,), jnp.float32, low / len(cuts), high / len(cuts))
        level = level * jnp.repeat(jnp.exp(draws), extent[dim] // shards_of).reshape((-1,) + (1,) * (len(extent) - 1 - dim))
    return level


def centred(own_key, extent, scale, limit, shards=(), kind=jnp.bfloat16):
    gain = steps_of(own_key, extent, shards, -0.22, 0.18) if shards else 1.0
    entries = jax.random.normal(own_key, extent, jnp.float32) * scale * gain
    return jnp.minimum(jnp.maximum(entries, -limit), limit).astype(kind)


def setup_inputs(seed: int = 0) -> dict:
    seeds = jax.random.split(jax.random.key(seed), 7)
    return {
        "queries": draw_queries(jax.random.fold_in(seeds[6], 71), 0),
        "key_rows": draw_key_rows(jax.random.fold_in(seeds[6], 71), 0),
        "value_rows": centred(seeds[2], (TOKENS, D), 1.0, 6.0, ((0, 64), (1, 4))),
        "out_weight": centred(seeds[3], (D, D), (max(D // 512, 1)) ** -0.5, 3.0, ((0, 4),)),
        "grad_out": centred(seeds[4], (TOKENS, D), 0.25, 1.5, ((0, 64), (1, 4))),
        "offsets": draw_offsets(jax.random.fold_in(seeds[6], 71), 0),
    }


def rounded(values):
    return lax.optimization_barrier(values.astype(jnp.bfloat16)).astype(jnp.float32)


def pick_rows(matrix, stride, offset):
    shaped = matrix.reshape((matrix.shape[0] // stride, stride) + matrix.shape[1:])
    return lax.dynamic_index_in_dim(shaped, offset, 1, keepdims=False)


def place_rows(values, stride, offset, filler):
    chosen = jnp.arange(stride, dtype=jnp.int32) == offset
    chosen = chosen.reshape((1, stride) + (1,) * (values.ndim - 1))
    spread = jnp.where(chosen, values[:, None], filler)
    return spread.reshape((values.shape[0] * stride,) + values.shape[1:])


def head_pass(inputs):
    query_head, key_head, value_head, grad_head, offset_trio = inputs
    score_scale = HEAD_DIM ** -0.5
    strides = (1, GROUP, N_SEQ)
    causal = jnp.arange(TOK_DEV)[:, None] >= jnp.arange(TOK_DEV)[None, :]
    saved = []
    row_max = jnp.full((TOKENS,), -jnp.inf, jnp.float32)
    for level_index in range(3):
        stride = strides[level_index]
        offset = offset_trio[level_index]
        query_seg = pick_rows(query_head, stride, offset).reshape(-1, TOK_DEV, HEAD_DIM).astype(jnp.float32)
        key_seg = pick_rows(key_head, stride, offset).reshape(-1, TOK_DEV, HEAD_DIM).astype(jnp.float32)
        value_seg = pick_rows(value_head, stride, offset).reshape(-1, TOK_DEV, HEAD_DIM).astype(jnp.float32)
        grad_seg = pick_rows(grad_head, stride, offset).reshape(-1, TOK_DEV, HEAD_DIM).astype(jnp.float32)
        scores = jnp.einsum("sid,sjd->sij", query_seg, key_seg) * score_scale
        scores = jnp.where(causal[None], scores, -jnp.inf)
        level_max = jnp.max(scores, -1).reshape(-1)
        row_max = jnp.maximum(row_max, place_rows(level_max, stride, offset, -jnp.inf))
        saved.append((stride, offset, query_seg, key_seg, value_seg, grad_seg, scores))
    totals = jnp.zeros((TOKENS,), jnp.float32)
    weighted = jnp.zeros((TOKENS, HEAD_DIM), jnp.float32)
    exps = []
    for level_index in range(3):
        stride, offset, query_seg, key_seg, value_seg, grad_seg, scores = saved[level_index]
        level_rowmax = pick_rows(row_max, stride, offset).reshape(-1, TOK_DEV)
        exp_scores = jnp.exp(scores - level_rowmax[..., None])
        totals = totals + place_rows(jnp.sum(exp_scores, -1).reshape(-1), stride, offset, 0.0)
        level_sum = jnp.einsum("sij,sjd->sid", rounded(exp_scores), value_seg)
        weighted = weighted + place_rows(level_sum.reshape(-1, HEAD_DIM), stride, offset, 0.0)
        exps.append(exp_scores)
    attended = (weighted / totals[:, None]).astype(jnp.bfloat16)
    attended_wide = lax.optimization_barrier(attended).astype(jnp.float32)
    row_inner = jnp.sum(grad_head.astype(jnp.float32) * attended_wide, -1)
    query_grad = jnp.zeros((TOKENS, HEAD_DIM), jnp.float32)
    key_grad = jnp.zeros((TOKENS, HEAD_DIM), jnp.float32)
    value_grad = jnp.zeros((TOKENS, HEAD_DIM), jnp.float32)
    for level_index in range(3):
        stride, offset, query_seg, key_seg, value_seg, grad_seg, scores = saved[level_index]
        exp_scores = exps[level_index]
        totals_seg = pick_rows(totals, stride, offset).reshape(-1, TOK_DEV)
        inner_seg = pick_rows(row_inner, stride, offset).reshape(-1, TOK_DEV)
        probability = exp_scores / totals_seg[..., None]
        value_term = jnp.einsum("sij,sid->sjd", rounded(probability), grad_seg)
        prob_grad = jnp.einsum("sid,sjd->sij", grad_seg, value_seg)
        score_grad = rounded(probability * (prob_grad - inner_seg[..., None]))
        query_term = score_scale * jnp.einsum("sij,sjd->sid", score_grad, key_seg)
        key_term = score_scale * jnp.einsum("sij,sid->sjd", score_grad, query_seg)
        query_grad = query_grad + place_rows(query_term.reshape(-1, HEAD_DIM), stride, offset, 0.0)
        key_grad = key_grad + place_rows(key_term.reshape(-1, HEAD_DIM), stride, offset, 0.0)
        value_grad = value_grad + place_rows(value_term.reshape(-1, HEAD_DIM), stride, offset, 0.0)
    return (attended, query_grad.astype(jnp.bfloat16), key_grad.astype(jnp.bfloat16),
            value_grad.astype(jnp.bfloat16))


def reference(queries, key_rows, value_rows, out_weight, grad_out, offsets):
    out_grad = jnp.dot(grad_out, out_weight.T, preferred_element_type=jnp.float32).astype(jnp.bfloat16)

    def by_head(matrix):
        return matrix.reshape(TOKENS, HEADS, HEAD_DIM).transpose(1, 0, 2)

    def by_token(stacked):
        return stacked.transpose(1, 0, 2).reshape(TOKENS, D)

    offset_trio = jnp.concatenate([jnp.zeros((1, HEADS), jnp.int32), offsets.astype(jnp.int32)], 0).T
    attended, query_grad, key_grad, value_grad = lax.map(
        head_pass, (by_head(queries), by_head(key_rows), by_head(value_rows), by_head(out_grad), offset_trio))
    mixed = jnp.dot(by_token(attended), out_weight, preferred_element_type=jnp.float32).astype(jnp.bfloat16)
    return mixed, by_token(query_grad), by_token(key_grad), by_token(value_grad)
```

```python
import functools

import jax
import jax.numpy as jnp
from jax import lax
from jax.experimental import pallas as pl
from jax.experimental.pallas import tpu as pltpu
from jax.sharding import PartitionSpec as P

MESH = pl.DeviceIdType.MESH
BF = jnp.bfloat16
F32 = jnp.float32
HD = 128
HEADS = 4
ROWS = 512
SCALE = HD ** (-0.5)
NY, NZ = 4, 8
NEG = -1e30


def nn(a, b):
    return lax.dot_general(a, b, (((1,), (0,)), ((), ())), preferred_element_type=F32)


def nt(a, b):
    return lax.dot_general(a, b, (((1,), (1,)), ((), ())), preferred_element_type=F32)


def tn(a, b):
    return lax.dot_general(a, b, (((0,), (0,)), ((), ())), preferred_element_type=F32)


def iota(shape, dim):
    return lax.broadcasted_iota(jnp.int32, shape, dim)


def low(x):
    return x.astype(BF)


def hi_lo(x):
    hi = x.astype(BF).astype(F32)
    return hi, x - hi


def kernel(offs, q, k, v, w, g, mixed, dq, dk, dv,
           gbuf, gacc, dot_, do_, nkv, fown, fx, fkv, e_l, e_n, e_f, o_l, o_n, o_f,
           st_l, st_n, st_f, q_n, q_f, a_n, a_f, att, c_l, c_n, c_f, inn, dqt, dka, dva,
           fgr, rz, ry, xs, xr, ng, nrb, mcs, mcr, mkeep, mxs, mxr,
           ss, rs, nss, nrs, gss, grs):
    s = lax.axis_index("seq")
    m = lax.axis_index("mp")
    y, z, xh = s // 16, (s // 2) % NZ, s % 2
    l, c = m // 2, m % 2
    pos = s % 4

    def dev(yy, zz, hh):
        return ((yy * NZ + zz) * 2 + hh, m)

    core = (s, l * 2 + 1 - c)
    across = (s, (1 - l) * 2 + c)
    xpart = dev(y, z, 1 - xh)
    zup = dev(y, (z + 1) % NZ, xh)
    zdn = dev(y, (z + NZ - 1) % NZ, xh)
    yps = [dev((y + d) % NY, z, xh) for d in range(1, NY)]
    diag = dev(y, z + 1 - 2 * (z % 2), 1 - xh)
    partners = [core, across, xpart, zup, zdn, diag] + yps

    barrier = pltpu.get_barrier_semaphore()
    for p in partners:
        pl.semaphore_signal(barrier, inc=1, device_id=p, device_id_type=MESH)

    def rc(src, dst, i, to):
        return pltpu.make_async_remote_copy(
            src_ref=src, dst_ref=dst, send_sem=ss.at[i], recv_sem=rs.at[i],
            device_id=to, device_id_type=MESH)

    def hc(h):
        return pl.ds(h * HD, HD)

    ia = iota((HD, ROWS), 0)
    ii = iota((HD, ROWS), 1)
    for h in range(HEADS):
        far = jnp.where((ii == 64 * ia + offs[1, h]) & (ia < 8), 1.0, 0.0).astype(BF)
        a_f[h] = far
        few = far[:16]
        fk = nn(few, k[:, hc(h)])
        fv = nn(few, v[:, hc(h)])
        fown[:, hc(h)] = low(jnp.concatenate([fk[:8], fv[:8]], 0))
    pl.semaphore_wait(barrier, len(partners))

    cx = rc(fown, fx, 0, xpart)
    cx.start()
    cg_core = rc(g, gbuf.at[0], 1, core)
    cg_x = rc(g, gbuf.at[1], 2, across)
    cg_x.start()
    cg_core.start()

    for h in range(HEADS):
        near = jnp.where(ii == 4 * ia + offs[0, h], 1.0, 0.0).astype(BF)
        a_n[h] = near
        nkv[pos, 0:128, hc(h)] = low(nn(near, k[:, hc(h)]))
        nkv[pos, 128:256, hc(h)] = low(nn(near, v[:, hc(h)]))
    for t in range(1, 4):
        @pl.when(t > pos)
        def _():
            nkv[t] = jnp.zeros((256, ROWS), BF)

    def near_copy(t):
        return pltpu.make_async_remote_copy(
            src_ref=nkv.at[pos], dst_ref=nkv.at[pos], send_sem=nss.at[t],
            recv_sem=nrs.at[pos], device_id=(s - pos + t, m), device_id_type=MESH)

    def near_recv(t):
        return pltpu.make_async_remote_copy(
            src_ref=nkv.at[t], dst_ref=nkv.at[t], send_sem=nss.at[t],
            recv_sem=nrs.at[t], device_id=(s - pos + t, m), device_id_type=MESH)

    for t in range(1, 4):
        @pl.when(t > pos)
        def _():
            near_copy(t).start()

    def local_fwd(h):
        for ib in range(2):
            nk = 256 * (ib + 1)
            qs = slice(ib * 256, ib * 256 + 256)
            st = nt(k[0:nk, hc(h)], q[qs, hc(h)]) * SCALE
            jj = iota((nk, 256), 0)
            qq = iota((nk, 256), 1) + ib * 256
            st = jnp.where(jj <= qq, st, NEG)
            mx = jnp.max(st, 0, keepdims=True).astype(BF).astype(F32)
            e = jnp.exp(st - mx)
            el = low(e)
            e_l[h, 0:nk, qs] = el
            o_l[h, :, qs] = tn(v[0:nk, hc(h)], el)
            st_l[h, 0:1, qs] = mx
            st_l[h, 1:2, qs] = jnp.sum(e, 0, keepdims=True)

    local_fwd(0)
    cx.wait()
    mine = fown[...].astype(F32)
    other = fx[...].astype(F32)
    first = jnp.where(xh == 0, mine, other)
    second = jnp.where(xh == 0, other, mine)
    fkv[z, y] = low(jnp.concatenate([first[:8], second[:8], first[8:], second[8:]], 0))
    cy = [rc(fkv.at[z, y], fkv.at[z, y], 4 + d, yps[d]) for d in range(3)]
    for cp in cy:
        cp.start()
    local_fwd(1)
    for cp in cy:
        cp.wait()

    def z_step(t):
        up = (z + NZ - t) % NZ
        dn = (z + t) % NZ
        if t < 3:
            a, b = fkv.at[up], fkv.at[dn]
        else:
            a, b = fkv.at[up, pl.ds(0, 2)], fkv.at[dn, pl.ds(2, 2)]
        return rc(a, a, 8 + t, zup), rc(b, b, 12 + t, zdn)

    zs = [z_step(t) for t in range(4)]

    def z_go(t):
        if t:
            zs[t - 1][0].wait_recv()
            zs[t - 1][1].wait_recv()
        if t < 4:
            zs[t][0].start()
            zs[t][1].start()

    def grad_part(slot):
        src = [(l, c), (l, 1 - c), (1 - l, c), (1 - l, 1 - c)][slot]
        cols = pl.ds(pl.multiple_of((src[0] * 2 + src[1]) * ROWS, ROWS), ROWS)
        part = nt(w[:, cols], g[...] if slot == 0 else gbuf[slot - 1])
        if slot:
            part = part + gacc[...]
        gacc[...] = part

    z_go(0)
    local_fwd(2)
    z_go(1)
    local_fwd(3)
    cg_core.wait()
    grad_part(0)
    z_go(2)
    grad_part(1)
    z_go(3)
    cg_x.wait()
    cg_f = rc(gbuf.at[1], gbuf.at[2], 3, core)
    cg_f.start()
    grad_part(2)
    cg_f.wait()
    grad_part(3)
    dot_[...] = low(gacc[...])
    do_[...] = low(gacc[...].T)

    def level_fwd(h, sel, kk, vv, seen, e_s, o_s, st_s, q_s):
        qq = low(nn(sel, q[:, hc(h)]))
        q_s[h] = qq
        st = nt(kk, qq) * SCALE
        st = jnp.where(seen, st, NEG)
        mx = jnp.max(st, 0, keepdims=True).astype(BF).astype(F32)
        e = jnp.exp(st - mx)
        el = low(e)
        e_s[h] = el
        o_s[h] = tn(vv, el)
        st_s[h, 0:1, :] = mx
        st_s[h, 1:2, :] = jnp.sum(e, 0, keepdims=True)

    jn = iota((ROWS, HD), 0)
    an = iota((ROWS, HD), 1)
    near_seen = jn <= pos * 128 + an
    key_index = ((jn // 16) % 4) * 128 + (jn // 64) * 16 + jn % 16
    far_seen = key_index <= s * 8 + an

    def near_k(h):
        return nkv[:, 0:128, hc(h)].reshape(ROWS, HD)

    def near_v(h):
        return nkv[:, 128:256, hc(h)].reshape(ROWS, HD)

    def far_k(h):
        return fkv[:, :, 0:16, hc(h)].reshape(ROWS, HD)

    def far_v(h):
        return fkv[:, :, 16:32, hc(h)].reshape(ROWS, HD)

    for t in range(3):
        @pl.when(t < pos)
        def _():
            near_recv(t).wait_recv()
    for h in range(HEADS):
        level_fwd(h, a_n[h], near_k(h), near_v(h), near_seen, e_n, o_n, st_n, q_n)
    z_go(4)
    for h in range(HEADS):
        level_fwd(h, a_f[h], far_k(h), far_v(h), far_seen, e_f, o_f, st_f, q_f)

    lane = iota((1, ROWS), 1)

    def spread(o_s, st_s, sel, h):
        top = st_s[h, 0:1, :]
        hi, lo = hi_lo(st_s[h, 1:2, :])
        rest = jnp.concatenate([top, hi, lo, jnp.zeros((13, HD), F32)], 0)
        both = nn(low(jnp.concatenate([o_s[h], rest], 0)), sel)
        return both[0:HD], both[HD:HD + 1], both[HD + 1:HD + 2] + both[HD + 2:HD + 3]

    def picked(cf, inner, sel):
        c_hi, c_lo = hi_lo(cf)
        i_hi, i_lo = hi_lo(inner)
        rows = jnp.concatenate([c_hi, c_lo, i_hi, i_lo, jnp.zeros((12, ROWS), F32)], 0)
        got = nt(low(rows), sel)
        return got[0:1] + got[1:2], got[2:3] + got[3:4]

    def combine(h):
        on, mn, sn = spread(o_n, st_n, a_n[h], h)
        of, mf, sf = spread(o_f, st_f, a_f[h], h)
        is_n = lane % 4 == offs[0, h]
        is_f = lane % 64 == offs[1, h]
        mn = jnp.where(is_n, mn, NEG)
        mf = jnp.where(is_f, mf, NEG)
        ml = st_l[h, 0:1, :]
        top = jnp.maximum(ml, jnp.maximum(mn, mf))
        wl, wn, wf = jnp.exp(ml - top), jnp.exp(mn - top), jnp.exp(mf - top)
        total = st_l[h, 1:2, :] * wl + sn * wn + sf * wf
        inv = 1.0 / total
        out = low((o_l[h] * wl + on * wn + of * wf) * inv)
        att[hc(h), :] = out
        inner = jnp.sum(dot_[hc(h), :].astype(F32) * out.astype(F32), 0, keepdims=True)
        c_l[h, 0:1, :] = wl * inv
        inn[h, 0:1, :] = inner
        cn, inner_n = picked(wn * inv, inner, a_n[h])
        cf, inner_f = picked(wf * inv, inner, a_f[h])
        c_n[h, 0:1, :] = cn
        c_n[h, 1:2, :] = inner_n
        c_f[h, 0:1, :] = cf
        c_f[h, 1:2, :] = inner_f

    for h in range(HEADS):
        combine(h)

    def level_bwd(h, sel, kk, vv, e_s, q_s, c_s):
        dd = low(nn(sel, do_[:, hc(h)]))
        prob = e_s[h].astype(F32) * c_s[h, 0:1, :]
        ds = low(prob * (nt(vv, dd) - c_s[h, 1:2, :]))
        return low(nn(ds, q_s[h]) * SCALE), low(nn(low(prob), dd)), nn(low(tn(kk, ds) * SCALE), sel)

    for h in range(HEADS):
        kt, vt, qt = level_bwd(h, a_f[h], far_k(h), far_v(h), e_f, q_f, c_f)
        fgr[:, :, 0:16, hc(h)] = kt.reshape(NZ, NY, 16, HD)
        fgr[:, :, 16:32, hc(h)] = vt.reshape(NZ, NY, 16, HD)
        dqt[h] = qt

    def rz_step(t):
        up = (z + 4 - t) % NZ
        dn = (z + 4 + t) % NZ
        if t:
            return (rc(fgr.at[up], rz.at[0, t], 16 + t, zup), rc(fgr.at[dn], rz.at[1, t], 20 + t, zdn))
        return (rc(fgr.at[up, pl.ds(0, 2)], rz.at[0, 0, pl.ds(0, 2)], 16, zup),
                rc(fgr.at[dn, pl.ds(2, 2)], rz.at[1, 0, pl.ds(2, 2)], 20, zdn))

    rzs = [rz_step(t) for t in range(4)]

    def add_block(dst, src):
        dst[...] = low(dst[...].astype(F32) + src[...].astype(F32))

    def rz_go(t):
        if t:
            rzs[t - 1][0].wait_recv()
            rzs[t - 1][1].wait_recv()
            up = (z + 4 - t) % NZ
            dn = (z + 4 + t) % NZ
            if t == 1:
                add_block(fgr.at[up, pl.ds(0, 2)], rz.at[0, 0, pl.ds(0, 2)])
                add_block(fgr.at[dn, pl.ds(2, 2)], rz.at[1, 0, pl.ds(2, 2)])
            elif t < 4:
                add_block(fgr.at[up], rz.at[0, t - 1])
                add_block(fgr.at[dn], rz.at[1, t - 1])
        if t < 4:
            rzs[t][0].start()
            rzs[t][1].start()

    rz_go(0)
    for h in range(HEADS):
        kt, vt, qt = level_bwd(h, a_n[h], near_k(h), near_v(h), e_n, q_n, c_n)
        ng[:, 0:128, hc(h)] = kt.reshape(4, HD, HD)
        ng[:, 128:256, hc(h)] = vt.reshape(4, HD, HD)
        dqt[h] = dqt[h] + qt

    def grad_copy(t):
        return pltpu.make_async_remote_copy(
            src_ref=ng.at[t], dst_ref=nrb.at[pos], send_sem=gss.at[t],
            recv_sem=grs.at[pos], device_id=(s - pos + t, m), device_id_type=MESH)

    def grad_recv(t):
        return pltpu.make_async_remote_copy(
            src_ref=ng.at[t], dst_ref=nrb.at[t], send_sem=gss.at[t],
            recv_sem=grs.at[t], device_id=(s - pos + t, m), device_id_type=MESH)

    for t in range(3):
        @pl.when(t < pos)
        def _():
            grad_copy(t).start()
    rz_go(1)

    def mixed_part(ll, cc):
        cols = pl.ds(pl.multiple_of((ll * 2 + cc) * ROWS, ROWS), ROWS)
        return tn(att[...], w[:, cols])

    mcs[0] = low(mixed_part(1 - l, 1 - c))
    cm0 = rc(mcs.at[0], mcr.at[0], 24, core)
    cm0.start()
    mkeep[...] = mixed_part(1 - l, c)
    cm0.wait()
    mxs[...] = low(mkeep[...] + mcr[0].astype(F32))
    cmx = rc(mxs, mxr, 25, across)
    cmx.start()
    rz_go(2)
    mcs[1] = low(mixed_part(l, 1 - c))
    cm1 = rc(mcs.at[1], mcr.at[1], 26, core)
    cm1.start()
    mkeep[...] = mixed_part(l, c)
    cm1.wait()
    mkeep[...] = mkeep[...] + mcr[1].astype(F32)

    def local_bwd(h):
        for ib in range(2):
            nk = 256 * (ib + 1)
            qs = slice(ib * 256, ib * 256 + 256)
            prob = e_l[h, 0:nk, qs].astype(F32) * c_l[h, 0:1, qs]
            dp = nn(v[0:nk, hc(h)], dot_[hc(h), qs])
            ds = low(prob * (dp - inn[h, 0:1, qs]))
            vt = nn(low(prob), do_[qs, hc(h)])
            kt = nn(ds, q[qs, hc(h)]) * SCALE
            if ib == 0:
                dva[0:nk, hc(h)] = vt
                dka[0:nk, hc(h)] = kt
            else:
                dva[0:256, hc(h)] = dva[0:256, hc(h)] + vt[0:256]
                dka[0:256, hc(h)] = dka[0:256, hc(h)] + kt[0:256]
                dva[256:512, hc(h)] = vt[256:512]
                dka[256:512, hc(h)] = kt[256:512]
            qt = tn(k[0:nk, hc(h)], ds) * SCALE + dqt[h, :, qs]
            dq[qs, hc(h)] = low(qt.T)

    local_bwd(0)
    local_bwd(1)
    rz_go(3)
    local_bwd(2)
    local_bwd(3)
    rz_go(4)
    total = fgr[z].astype(F32) + rz[0, 3].astype(F32) + rz[1, 3].astype(F32)
    fgr[z] = low(total)
    cry = [rc(fgr.at[z, (y + d + 1) % NY], ry.at[d], 28 + d, yps[d]) for d in range(3)]
    for cp in cry:
        cp.start()
    for t in range(1, 4):
        @pl.when(t > pos)
        def _():
            grad_recv(t).wait_recv()
            add_block(ng.at[pos], nrb.at[t])
    jt = iota((ROWS, HD), 0)
    at = iota((ROWS, HD), 1)
    for h in range(HEADS):
        back = jnp.where(jt == 4 * at + offs[0, h], 1.0, 0.0).astype(BF)
        dka[:, hc(h)] = dka[:, hc(h)] + nn(back, ng[pos, 0:128, hc(h)])
        dva[:, hc(h)] = dva[:, hc(h)] + nn(back, ng[pos, 128:256, hc(h)])
    for cp in cry:
        cp.wait()
    total = fgr[z, y].astype(F32)
    for d in range(3):
        total = total + ry[d].astype(F32)
    low_half = jnp.concatenate([total[0:8], total[16:24]], 0)
    high_half = jnp.concatenate([total[8:16], total[24:32]], 0)
    xs[...] = low(jnp.where(xh == 0, high_half, low_half))
    cxr = rc(xs, xr, 27, xpart)
    cxr.start()
    cmx.wait()
    mixed[...] = low(mkeep[...] + mxr[...].astype(F32))
    cxr.wait()
    far_sum = jnp.where(xh == 0, low_half, high_half) + xr[...].astype(F32)
    far_key = low(jnp.concatenate([far_sum[0:8], jnp.zeros((8, ROWS), F32)], 0))
    far_val = low(jnp.concatenate([far_sum[8:16], jnp.zeros((8, ROWS), F32)], 0))
    jf = iota((ROWS, 16), 0)
    af = iota((ROWS, 16), 1)
    for h in range(HEADS):
        back = jnp.where((jf == 64 * af + offs[1, h]) & (af < 8), 1.0, 0.0).astype(BF)
        dk[:, hc(h)] = low(dka[:, hc(h)] + nn(back, far_key[:, h * HD:(h + 1) * HD]))
        dv[:, hc(h)] = low(dva[:, hc(h)] + nn(back, far_val[:, h * HD:(h + 1) * HD]))

    for t in range(4):
        zs[t][0].wait_send()
        zs[t][1].wait_send()
        rzs[t][0].wait_send()
        rzs[t][1].wait_send()
    for t in range(1, 4):
        @pl.when(t > pos)
        def _():
            near_copy(t).wait_send()
    for t in range(3):
        @pl.when(t < pos)
        def _():
            grad_copy(t).wait_send()


def local(queries, key_rows, value_rows, out_weight, grad_out, offsets):
    vm = pl.BlockSpec(memory_space=pltpu.VMEM)
    shape = jax.ShapeDtypeStruct((ROWS, ROWS), BF)
    V = pltpu.VMEM
    dma = pltpu.SemaphoreType.DMA
    return pl.pallas_call(
        kernel,
        out_shape=(shape,) * 4,
        in_specs=[pl.BlockSpec(memory_space=pltpu.SMEM)] + [vm] * 5,
        out_specs=(vm,) * 4,
        scratch_shapes=[
            V((3, ROWS, ROWS), BF), V((ROWS, ROWS), F32), V((ROWS, ROWS), BF), V((ROWS, ROWS), BF),
            V((4, 256, ROWS), BF), V((16, ROWS), BF), V((16, ROWS), BF), V((NZ, NY, 32, ROWS), BF),
            V((HEADS, ROWS, ROWS), BF), V((HEADS, ROWS, HD), BF), V((HEADS, ROWS, HD), BF),
            V((HEADS, HD, ROWS), F32), V((HEADS, HD, HD), F32), V((HEADS, HD, HD), F32),
            V((HEADS, 8, ROWS), F32), V((HEADS, 8, HD), F32), V((HEADS, 8, HD), F32),
            V((HEADS, HD, HD), BF), V((HEADS, HD, HD), BF),
            V((HEADS, HD, ROWS), BF), V((HEADS, HD, ROWS), BF),
            V((ROWS, ROWS), BF),
            V((HEADS, 8, ROWS), F32), V((HEADS, 8, HD), F32), V((HEADS, 8, HD), F32), V((HEADS, 8, ROWS), F32),
            V((HEADS, HD, ROWS), F32), V((ROWS, ROWS), F32), V((ROWS, ROWS), F32),
            V((NZ, NY, 32, ROWS), BF), V((2, 4, NY, 32, ROWS), BF), V((3, 32, ROWS), BF),
            V((16, ROWS), BF), V((16, ROWS), BF),
            V((4, 256, ROWS), BF), V((4, 256, ROWS), BF),
            V((2, ROWS, ROWS), BF), V((2, ROWS, ROWS), BF), V((ROWS, ROWS), F32),
            V((ROWS, ROWS), BF), V((ROWS, ROWS), BF),
            dma((32,)), dma((32,)), dma((4,)), dma((4,)), dma((4,)), dma((4,)),
        ],
        compiler_params=pltpu.CompilerParams(
            collective_id=0, has_side_effects=True, vmem_limit_bytes=56 << 20),
        cost_estimate=pl.CostEstimate(flops=4_400_000_000, bytes_accessed=8 << 20, transcendentals=1_400_000),
        name="dilated",
    )(offsets, queries, key_rows, value_rows, out_weight, grad_out)


def solution(mesh):
    return jax.shard_map(
        local,
        mesh=mesh,
        in_specs=(
            P("seq", "mp"),
            P("seq", "mp"),
            P("seq", "mp"),
            P("mp", None),
            P("seq", "mp"),
            P(None, "mp"),
        ),
        out_specs=(P("seq", "mp"), P("seq", "mp"), P("seq", "mp"), P("seq", "mp")),
        check_vma=False,
    )
```

```python
import functools

import jax
import jax.numpy as jnp
from jax import lax
from jax.experimental import pallas as pl
from jax.experimental.pallas import tpu as pltpu
from jax.sharding import PartitionSpec as P

MESH = pl.DeviceIdType.MESH
BF = jnp.bfloat16
F32 = jnp.float32
HD = 128
HEADS = 4
ROWS = 512
SCALE = HD ** (-0.5)
NY, NZ = 4, 8
NEG = -1e30


def nn(a, b):
    return lax.dot_general(a, b, (((1,), (0,)), ((), ())), preferred_element_type=F32)


def nt(a, b):
    return lax.dot_general(a, b, (((1,), (1,)), ((), ())), preferred_element_type=F32)


def tn(a, b):
    return lax.dot_general(a, b, (((0,), (0,)), ((), ())), preferred_element_type=F32)


def iota(shape, dim):
    return lax.broadcasted_iota(jnp.int32, shape, dim)


def low(x):
    return x.astype(BF)


def hi_lo(x):
    hi = x.astype(BF).astype(F32)
    return hi, x - hi


def kernel(offs, qh, kh, vh, wh, gh, mixed, dq, dk, dv,
           q, k, v, w, g, gbuf, gacc, dot_, do_, nkv, e_l, e_n, e_f, o_l, o_n,
           st_l, st_n, q_n, a_n, a_f, f16, att, c_l, c_n, inn, dqt, dqa, dka, dva,
           p1s, p1r, fkv, fo, p5s, p5r, fgr, rz, p8s, p8r,
           ng, nrb, mcs, mcr, mkeep, mxs, mxr,
           ins, ss, rs):
    s = lax.axis_index("seq")
    m = lax.axis_index("mp")
    y, z, xh = s // 16, (s // 2) % NZ, s % 2
    l, c = m // 2, m % 2
    pos = s % 4

    def dev(yy, zz, hh):
        return ((yy * NZ + zz) * 2 + hh, m)

    core = (s, l * 2 + 1 - c)
    across = (s, (1 - l) * 2 + c)
    xpart = dev(y, z, 1 - xh)
    zpart = dev(y, z + 1 - 2 * (z % 2), xh)
    ys = [(y + d) % NY for d in range(1, NY)]
    yps = [dev(yy, z, xh) for yy in ys]
    zps = [dev(y, (z + d) % NZ, xh) for d in range(1, NZ)]
    yx = [((y + n // 2) % NY, (xh + n % 2) % 2) for n in range(1, 2 * NY)]
    partners = [core, across] + [dev(yy, z, hh) for yy, hh in yx] + zps

    barrier = pltpu.get_barrier_semaphore()
    for p in partners:
        pl.semaphore_signal(barrier, inc=1, device_id=p, device_id_type=MESH)
    loads = [pltpu.make_async_copy(a, b, ins.at[i])
             for i, (a, b) in enumerate([(kh, k), (vh, v), (qh, q), (gh, g), (wh, w)])]
    for cp in loads:
        cp.start()

    def rc(src, dst, i, to):
        return pltpu.make_async_remote_copy(
            src_ref=src, dst_ref=dst, send_sem=ss.at[i], recv_sem=rs.at[i],
            device_id=to, device_id_type=MESH)

    def hc(h):
        return pl.ds(h * HD, HD)

    ia = iota((HD, ROWS), 0)
    ii = iota((HD, ROWS), 1)
    for h in range(HEADS):
        a_n[h] = jnp.where(ii == 4 * ia + offs[0, h], 1.0, 0.0).astype(BF)
        fa = ia - 8 * y
        a_f[h] = jnp.where((ii == 64 * fa + offs[1, h]) & (fa >= 0) & (fa < 8), 1.0, 0.0).astype(BF)
        f16[h] = jnp.where((ii[:16] == 64 * ia[:16] + offs[1, h]) & (ia[:16] < 8), 1.0, 0.0).astype(BF)
    for cp in loads[:3]:
        cp.wait()
    pad8 = jnp.zeros((8, HD), F32)
    for h in range(HEADS):
        rows = [nn(f16[h], x[:, hc(h)])[:8] for x in (k, v, q)]
        p1s[h] = low(jnp.concatenate(rows + [pad8], 0))
    for h in range(HEADS):
        nkv[pos, 0:128, hc(h)] = low(nn(a_n[h], k[:, hc(h)]))
        nkv[pos, 128:256, hc(h)] = low(nn(a_n[h], v[:, hc(h)]))
    for t in range(1, 4):
        @pl.when(t > pos)
        def _():
            nkv[t] = jnp.zeros((256, ROWS), BF)

    def near_send(base, slot, to):
        return [rc(nkv.at[slot, pl.ds(128 * n, 128)], nkv.at[slot, pl.ds(128 * n, 128)], base + n, to)
                for n in range(2)]

    z_even = z % 2 == 0
    near_z = near_send(40, pos, zpart)
    near_x = near_send(42, pos, xpart)
    relay_z = near_send(44, 0, zpart)
    relay_x = near_send(44, 1, xpart)

    def local_fwd(h):
        for ib in range(2):
            nk = 256 * (ib + 1)
            qs = slice(ib * 256, ib * 256 + 256)
            st = nt(k[0:nk, hc(h)], q[qs, hc(h)]) * SCALE
            jj = iota((nk, 256), 0)
            qq = iota((nk, 256), 1) + ib * 256
            st = jnp.where(jj <= qq, st, NEG)
            mx = jnp.max(st, 0, keepdims=True).astype(BF).astype(F32)
            e = jnp.exp(st - mx)
            el = low(e)
            e_l[h, 0:nk, qs] = el
            o_l[h, :, qs] = tn(v[0:nk, hc(h)], el)
            st_l[h, 0:1, qs] = mx
            st_l[h, 1:2, qs] = jnp.sum(e, 0, keepdims=True)

    local_fwd(0)
    local_fwd(1)
    loads[3].wait()
    pl.semaphore_wait(barrier, len(partners))

    p1 = [rc(p1s.at[yx[n][0]], p1r.at[xh, y], n, dev(yx[n][0], z, yx[n][1])) for n in range(7)]
    for cp in p1:
        cp.start()
    p1r[xh, y] = p1s[y]

    @pl.when(xh == 0)
    def _():
        for cp in near_x:
            cp.start()

    @pl.when(z_even)
    def _():
        for cp in near_z:
            cp.start()

    def halves(src, dst, base, to):
        return [rc(src.at[pl.ds(256 * n, 256)], dst.at[pl.ds(256 * n, 256)], base + n, to) for n in range(2)]

    cg_x = halves(g, gbuf.at[1], 50, across)
    cg_core = rc(g, gbuf.at[0], 28, core)
    cg_f = halves(gbuf.at[1], gbuf.at[2], 52, core)
    for cp in cg_x:
        cp.start()
    cg_core.start()
    local_fwd(2)
    local_fwd(3)
    for cp in p1:
        cp.wait()
    for hh in range(2):
        got = [p1r[hh, t].astype(F32) for t in range(NY)]
        fkv[z, hh] = low(jnp.concatenate([x[0:8] for x in got] + [x[8:16] for x in got], 0))
    p3 = [rc(fkv.at[z], fkv.at[z], 7 + d, zps[d]) for d in range(7)]
    for d in (3, 2, 4, 1, 5, 0, 6):
        p3[d].start()
    got = [p1r[xh, t].astype(F32) for t in range(NY)]
    fq = low(jnp.concatenate([x[16:24] for x in got] + [jnp.zeros((96, HD), F32)], 0))

    def grad_part(slot):
        src = [(l, c), (l, 1 - c), (1 - l, c), (1 - l, 1 - c)][slot]
        cols = pl.ds(pl.multiple_of((src[0] * 2 + src[1]) * ROWS, ROWS), ROWS)
        part = nt(w[:, cols], g[...] if slot == 0 else gbuf[slot - 1])
        if slot:
            part = part + gacc[...]
        gacc[...] = part

    loads[4].wait()
    grad_part(0)
    cg_core.wait()
    grad_part(1)

    @pl.when(pos == 1)
    def _():
        for n in range(2):
            near_x[n].wait_recv()
            relay_z[n].start()

    @pl.when(pos == 3)
    def _():
        for n in range(2):
            near_z[n].wait_recv()
            relay_x[n].start()

    def scores(kk, qq, vv, seen):
        st = nt(kk, qq) * SCALE
        st = jnp.where(seen, st, NEG)
        mx = jnp.max(st, 0, keepdims=True).astype(BF).astype(F32)
        e = jnp.exp(st - mx)
        el = low(e)
        hi, lo = hi_lo(jnp.sum(e, 0, keepdims=True))
        return el, low(jnp.concatenate([tn(vv, el), mx, hi, lo, jnp.zeros((13, HD), F32)], 0))

    jn = iota((ROWS, HD), 0)
    an = iota((ROWS, HD), 1)
    near_seen = jn <= pos * 128 + an
    key_index = ((jn // 8) % 4) * 128 + (jn // 64) * 16 + ((jn // 32) % 2) * 8 + jn % 8
    query_index = (an // 8) * 128 + z * 16 + xh * 8 + an % 8
    far_seen = key_index <= query_index

    def near_k(h):
        return nkv[:, 0:128, hc(h)].reshape(ROWS, HD)

    def near_v(h):
        return nkv[:, 128:256, hc(h)].reshape(ROWS, HD)

    for cp in p3:
        cp.wait_recv()
    far_k = fkv[:, :, 0:32, :].reshape(ROWS, HD)
    far_v = fkv[:, :, 32:64, :].reshape(ROWS, HD)
    el, block = scores(far_k, fq, far_v, far_seen)
    e_f[...] = el
    fo[y] = block
    p4 = [rc(fo.at[y], fo.at[y], 14 + d, yps[d]) for d in range(3)]
    for cp in p4:
        cp.start()

    for n in range(2):
        cg_x[n].wait()
        cg_f[n].start()
    grad_part(2)
    for n in range(2):
        cg_f[n].wait()
    grad_part(3)
    dot_[...] = low(gacc[...])
    do_[...] = low(gacc[...].T)

    @pl.when(pos == 2)
    def _():
        for n in range(2):
            near_z[n].wait_recv()
            relay_x[n].wait_recv()

    @pl.when(pos == 3)
    def _():
        for n in range(2):
            near_x[n].wait_recv()
            relay_z[n].wait_recv()

    for h in range(HEADS):
        qq = low(nn(a_n[h], q[:, hc(h)]))
        q_n[h] = qq
        el, block = scores(near_k(h), qq, near_v(h), near_seen)
        e_n[h] = el
        o_n[h] = block

    lane = iota((1, ROWS), 1)

    def spread(block, sel):
        both = nn(block, sel)
        return both[0:HD], both[HD:HD + 1], both[HD + 1:HD + 2] + both[HD + 2:HD + 3]

    def picked(cf, inner, sel):
        c_hi, c_lo = hi_lo(cf)
        i_hi, i_lo = hi_lo(inner)
        rows = jnp.concatenate([c_hi, c_lo, i_hi, i_lo, jnp.zeros((12, ROWS), F32)], 0)
        return nt(low(rows), sel)

    def combine(h):
        on, mn, sn = spread(o_n[h], a_n[h])
        of, mf, sf = spread(fo[h], a_f[h])
        mn = jnp.where(lane % 4 == offs[0, h], mn, NEG)
        mf = jnp.where(lane % 64 == offs[1, h], mf, NEG)
        ml = st_l[h, 0:1, :]
        top = jnp.maximum(ml, jnp.maximum(mn, mf))
        wl, wn, wf = jnp.exp(ml - top), jnp.exp(mn - top), jnp.exp(mf - top)
        total = st_l[h, 1:2, :] * wl + sn * wn + sf * wf
        inv = 1.0 / total
        out = low((o_l[h] * wl + on * wn + of * wf) * inv)
        att[hc(h), :] = out
        inner = jnp.sum(dot_[hc(h), :].astype(F32) * out.astype(F32), 0, keepdims=True)
        c_l[h, 0:1, :] = wl * inv
        inn[h, 0:1, :] = inner
        far = picked(wf * inv, inner, a_f[h])
        p5s[h] = low(jnp.concatenate([nn(f16[h], do_[:, hc(h)])[:8], far[:8]], 0))
        c_n[h] = picked(wn * inv, inner, a_n[h])

    for cp in p4:
        cp.wait()
    for h in range(HEADS):
        combine(h)
    p5 = [rc(p5s.at[ys[d]], p5r.at[y], 17 + d, yps[d]) for d in range(3)]
    for cp in p5:
        cp.start()
    p5r[y] = p5s[y]

    def mixed_part(ll, cc, n):
        cols = pl.ds(pl.multiple_of((ll * 2 + cc) * ROWS, ROWS), ROWS)
        return tn(att[:, 256 * n:256 * n + 256], w[:, cols])

    def half(n):
        return pl.ds(256 * n, 256)

    cm0 = halves(mcs.at[0], mcr.at[0], 54, core)
    cm1 = halves(mcs.at[1], mcr.at[1], 56, core)
    cmx = halves(mxs, mxr, 58, across)
    for n in range(2):
        mcs[0, half(n), :] = low(mixed_part(1 - l, 1 - c, n))
        cm0[n].start()
    for n in range(2):
        part = mixed_part(1 - l, c, n)
        cm0[n].wait()
        mxs[half(n), :] = low(part + mcr[0, half(n), :].astype(F32))
        cmx[n].start()

    for cp in p5:
        cp.wait()
    got = [p5r[t].astype(F32) for t in range(NY)]
    fd = low(jnp.concatenate([x[0:8] for x in got] + [jnp.zeros((96, HD), F32)], 0))
    stat = got[0][8:16] + got[1][8:16] + got[2][8:16] + got[3][8:16]
    far_k = fkv[:, :, 0:32, :].reshape(ROWS, HD)
    far_v = fkv[:, :, 32:64, :].reshape(ROWS, HD)
    prob = e_f[...].astype(F32) * (stat[0:1] + stat[1:2])
    ds = low(prob * (nt(far_v, fd) - (stat[2:3] + stat[3:4])))
    fgr[:, :, 0:32, :] = low(nn(ds, fq) * SCALE).reshape(NZ, 2, 32, HD)
    fgr[:, :, 32:64, :] = low(nn(low(prob), fd)).reshape(NZ, 2, 32, HD)
    p6 = [rc(fgr.at[(z + d + 1) % NZ], rz.at[d], 20 + d, zps[d]) for d in range(7)]
    for d in (3, 2, 4, 1, 5, 0, 6):
        p6[d].start()
    fdq = tn(ds, far_k)[0:32] * SCALE

    def near_bwd(h):
        dd = low(nn(a_n[h], do_[:, hc(h)]))
        prob = e_n[h].astype(F32) * (c_n[h, 0:1, :] + c_n[h, 1:2, :])
        ds = low(prob * (nt(near_v(h), dd) - (c_n[h, 2:3, :] + c_n[h, 3:4, :])))
        ng[:, 0:128, hc(h)] = low(nn(ds, q_n[h]) * SCALE).reshape(4, HD, HD)
        ng[:, 128:256, hc(h)] = low(nn(low(prob), dd)).reshape(4, HD, HD)
        dqt[h] = nn(low(tn(near_k(h), ds) * SCALE), a_n[h])

    for h in range(HEADS):
        near_bwd(h)

    back_z = rc(ng.at[0], nrb.at[0], 46, zpart)
    back_x = rc(ng.at[(pos + 3) % 4], nrb.at[1], 47, xpart)
    back_rx = rc(ng.at[0], nrb.at[2], 48, xpart)
    back_rz = rc(ng.at[1], nrb.at[2], 48, zpart)

    @pl.when(z % 2 == 1)
    def _():
        back_x.start()
        back_z.start()

    for cp in p6:
        cp.wait_recv()
    total = fgr[z].astype(F32)
    for d in range(7):
        total = total + rz[d].astype(F32)
    fgr[z] = low(total)
    for hh in range(2):
        for t in range(NY):
            r = slice(8 * t, 8 * t + 8)
            third = jnp.where(xh == hh, fdq[r], 0.0)
            p8s[hh, t] = low(jnp.concatenate(
                [total[hh, r], total[hh, 32 + 8 * t:40 + 8 * t], third, pad8], 0))
    p8 = [rc(p8s.at[yx[n][1], yx[n][0]], p8r.at[xh, y], 29 + n, dev(yx[n][0], z, yx[n][1])) for n in range(7)]
    for cp in p8:
        cp.start()
    p8r[xh, y] = p8s[xh, y]

    def add_block(dst, src):
        dst[...] = low(dst[...].astype(F32) + src[...].astype(F32))

    @pl.when(pos == 1)
    def _():
        back_z.wait_recv()
        add_block(ng.at[0], nrb.at[0])
        back_rx.start()

    @pl.when(pos == 3)
    def _():
        back_x.wait_recv()
        add_block(ng.at[1], nrb.at[1])
        back_rz.start()

    for n in range(2):
        mcs[1, half(n), :] = low(mixed_part(l, 1 - c, n))
        cm1[n].start()
    for n in range(2):
        mkeep[half(n), :] = mixed_part(l, c, n)

    def local_bwd(h):
        for ib in range(2):
            nk = 256 * (ib + 1)
            qs = slice(ib * 256, ib * 256 + 256)
            prob = e_l[h, 0:nk, qs].astype(F32) * c_l[h, 0:1, qs]
            dp = nn(v[0:nk, hc(h)], dot_[hc(h), qs])
            ds = low(prob * (dp - inn[h, 0:1, qs]))
            vt = nn(low(prob), do_[qs, hc(h)])
            kt = nn(ds, q[qs, hc(h)]) * SCALE
            if ib == 0:
                dva[0:nk, hc(h)] = vt
                dka[0:nk, hc(h)] = kt
            else:
                dva[0:256, hc(h)] = dva[0:256, hc(h)] + vt[0:256]
                dka[0:256, hc(h)] = dka[0:256, hc(h)] + kt[0:256]
                dva[256:512, hc(h)] = vt[256:512]
                dka[256:512, hc(h)] = kt[256:512]
            qt = tn(k[0:nk, hc(h)], ds) * SCALE + dqt[h, :, qs]
            dqa[qs, hc(h)] = qt.T

    for h in range(HEADS):
        local_bwd(h)
    for n in range(2):
        cm1[n].wait()
        cmx[n].wait()
        mixed[half(n), :] = low(mkeep[half(n), :] + mcr[1, half(n), :].astype(F32) + mxr[half(n), :].astype(F32))

    @pl.when(pos == 0)
    def _():
        back_z.wait_recv()
        add_block(ng.at[0], nrb.at[0])
        back_rx.wait_recv()
        add_block(ng.at[0], nrb.at[2])

    @pl.when(pos == 1)
    def _():
        back_rz.wait_recv()
        add_block(ng.at[1], nrb.at[2])

    @pl.when(pos == 2)
    def _():
        back_x.wait_recv()
        add_block(ng.at[2], nrb.at[1])

    for cp in p8:
        cp.wait()
    jt = iota((ROWS, HD), 0)
    at = iota((ROWS, HD), 1)
    jf = iota((ROWS, 16), 0)
    af = iota((ROWS, 16), 1)
    for h in range(HEADS):
        back_n = jnp.where(jt == 4 * at + offs[0, h], 1.0, 0.0).astype(BF)
        back_f = jnp.where((jf == 64 * af + offs[1, h]) & (af < 8), 1.0, 0.0).astype(BF)
        x = p8r[0, h].astype(F32) + p8r[1, h].astype(F32)
        wide = jnp.concatenate([x[0:8], x[8:16], x[16:24]], 1)
        far = nn(back_f, low(jnp.concatenate([wide, jnp.zeros((8, 3 * HD), F32)], 0)))
        dk[:, hc(h)] = low(dka[:, hc(h)] + nn(back_n, ng[pos, 0:128, hc(h)]) + far[:, 0:HD])
        dv[:, hc(h)] = low(dva[:, hc(h)] + nn(back_n, ng[pos, 128:256, hc(h)]) + far[:, HD:2 * HD])
        dq[:, hc(h)] = low(dqa[:, hc(h)] + far[:, 2 * HD:])

    for cp in p3 + p6:
        cp.wait_send()

    @pl.when(xh == 0)
    def _():
        for cp in near_x:
            cp.wait_send()

    @pl.when(z_even)
    def _():
        for cp in near_z:
            cp.wait_send()

    @pl.when(pos == 1)
    def _():
        for cp in relay_z:
            cp.wait_send()
        back_rx.wait_send()

    @pl.when(pos == 3)
    def _():
        for cp in relay_x:
            cp.wait_send()
        back_rz.wait_send()

    @pl.when(z % 2 == 1)
    def _():
        back_x.wait_send()
        back_z.wait_send()


def hand_on(a, b, c, d, a2, b2, c2, d2, hold, in_sem, out_sem):
    pairs = [(a, a2), (b, b2), (c, c2), (d, d2)]
    ins = [pltpu.make_async_copy(x, hold.at[j], in_sem.at[j]) for j, (x, _) in enumerate(pairs)]
    outs = [pltpu.make_async_copy(hold.at[j], x, out_sem.at[j]) for j, (_, x) in enumerate(pairs)]
    for cp in ins:
        cp.start()
    for i, o in zip(ins, outs):
        i.wait()
        o.start()
    for cp in outs:
        cp.wait()


def local(queries, key_rows, value_rows, out_weight, grad_out, offsets):
    vm = pl.BlockSpec(memory_space=pltpu.VMEM)
    hbm = pl.BlockSpec(memory_space=pl.ANY)
    shape = jax.ShapeDtypeStruct((ROWS, ROWS), BF)
    V = pltpu.VMEM
    dma = pltpu.SemaphoreType.DMA
    wide = (ROWS, ROWS)
    outs = pl.pallas_call(
        kernel,
        out_shape=(shape,) * 4,
        in_specs=[pl.BlockSpec(memory_space=pltpu.SMEM)] + [hbm] * 5,
        out_specs=(vm,) * 4,
        scratch_shapes=[
            V(wide, BF), V(wide, BF), V(wide, BF), V((ROWS, 4 * ROWS), BF), V(wide, BF),
            V((3, ROWS, ROWS), BF), V(wide, F32), V(wide, BF), V(wide, BF),
            V((4, 256, ROWS), BF),
            V((HEADS, ROWS, ROWS), BF), V((HEADS, ROWS, HD), BF), V((ROWS, HD), BF),
            V((HEADS, HD, ROWS), F32), V((HEADS, 144, HD), BF),
            V((HEADS, 8, ROWS), F32), V((HEADS, 8, HD), F32),
            V((HEADS, HD, HD), BF),
            V((HEADS, HD, ROWS), BF), V((HEADS, HD, ROWS), BF), V((HEADS, 16, ROWS), BF),
            V(wide, BF),
            V((HEADS, 8, ROWS), F32), V((HEADS, 16, HD), F32), V((HEADS, 8, ROWS), F32),
            V((HEADS, HD, ROWS), F32), V(wide, F32), V(wide, F32), V(wide, F32),
            V((NY, 32, HD), BF), V((2, NY, 32, HD), BF), V((NZ, 2, 64, HD), BF), V((NY, 144, HD), BF),
            V((NY, 16, HD), BF), V((NY, 16, HD), BF), V((NZ, 2, 64, HD), BF), V((NZ - 1, 2, 64, HD), BF),
            V((2, NY, 32, HD), BF), V((2, NY, 32, HD), BF),
            V((4, 256, ROWS), BF), V((3, 256, ROWS), BF),
            V((2, ROWS, ROWS), BF), V((2, ROWS, ROWS), BF), V(wide, F32),
            V(wide, BF), V(wide, BF),
            dma((5,)), dma((60,)), dma((60,)),
        ],
        compiler_params=pltpu.CompilerParams(
            collective_id=0, has_side_effects=True, vmem_limit_bytes=56 << 20),
        cost_estimate=pl.CostEstimate(flops=4_400_000_000, bytes_accessed=8 << 20, transcendentals=1_400_000),
        name="dilated",
    )(offsets, queries, key_rows, value_rows, out_weight, grad_out)
    return pl.pallas_call(
        hand_on,
        out_shape=(shape,) * 4,
        in_specs=[hbm] * 4,
        out_specs=(hbm,) * 4,
        scratch_shapes=[V((4, ROWS, ROWS), BF), dma((4,)), dma((4,))],
        name="hand_on",
    )(*outs)


def solution(mesh):
    return jax.shard_map(
        local,
        mesh=mesh,
        in_specs=(
            P("seq", "mp"),
            P("seq", "mp"),
            P("seq", "mp"),
            P("mp", None),
            P("seq", "mp"),
            P(None, "mp"),
        ),
        out_specs=(P("seq", "mp"), P("seq", "mp"), P("seq", "mp"), P("seq", "mp")),
        check_vma=False,
    )
```

```python
import functools

import jax
import jax.numpy as jnp
from jax import lax
from jax.experimental import pallas as pl
from jax.experimental.pallas import tpu as pltpu
from jax.sharding import PartitionSpec as P

MESH = pl.DeviceIdType.MESH
BF = jnp.bfloat16
F32 = jnp.float32
HD = 128
HEADS = 4
ROWS = 512
SCALE = HD ** (-0.5)
NY, NZ = 4, 8
NEG = -1e30


def nn(a, b):
    return lax.dot_general(a, b, (((1,), (0,)), ((), ())), preferred_element_type=F32)


def nt(a, b):
    return lax.dot_general(a, b, (((1,), (1,)), ((), ())), preferred_element_type=F32)


def tn(a, b):
    return lax.dot_general(a, b, (((0,), (0,)), ((), ())), preferred_element_type=F32)


def iota(shape, dim):
    return lax.broadcasted_iota(jnp.int32, shape, dim)


def low(x):
    return x.astype(BF)


def hi_lo(x):
    hi = x.astype(BF).astype(F32)
    return hi, x - hi


def kernel(offs, qh, kh, vh, wh, gh, mixed_h, dq_h, dk_h, dv_h, mixed, dq, dk, dv,
           q, k, v, w, g, gbuf, gacc, dot_, do_, nkv, e_l, e_n, e_f, o_l, o_n,
           st_l, st_n, q_n, a_n, a_f, f16, att, c_l, c_n, inn, dqt, dqa, dka, dva,
           p1s, p1r, fkv, fo, p5s, p5r, fgr, rz, p8s, p8r,
           ng, nrb, mcs, mcr, mkeep, mxs, mxr,
           back_n, back_f, ins, outs, ss, rs):
    s = lax.axis_index("seq")
    m = lax.axis_index("mp")
    y, z, xh = s // 16, (s // 2) % NZ, s % 2
    l, c = m // 2, m % 2
    pos = s % 4

    def dev(yy, zz, hh):
        return ((yy * NZ + zz) * 2 + hh, m)

    core = (s, l * 2 + 1 - c)
    across = (s, (1 - l) * 2 + c)
    xpart = dev(y, z, 1 - xh)
    zpart = dev(y, z + 1 - 2 * (z % 2), xh)
    ys = [(y + d) % NY for d in range(1, NY)]
    yps = [dev(yy, z, xh) for yy in ys]
    zps = [dev(y, (z + d) % NZ, xh) for d in range(1, NZ)]
    yx = [((y + n // 2) % NY, (xh + n % 2) % 2) for n in range(1, 2 * NY)]
    partners = [core, across] + [dev(yy, z, hh) for yy, hh in yx] + zps

    barrier = pltpu.get_barrier_semaphore()
    for p in partners:
        pl.semaphore_signal(barrier, inc=1, device_id=p, device_id_type=MESH)
    loads = [pltpu.make_async_copy(a, b, ins.at[i])
             for i, (a, b) in enumerate([(kh, k), (vh, v), (qh, q), (gh, g), (wh, w)])]
    for cp in loads:
        cp.start()

    def rc(src, dst, i, to):
        return pltpu.make_async_remote_copy(
            src_ref=src, dst_ref=dst, send_sem=ss.at[i], recv_sem=rs.at[i],
            device_id=to, device_id_type=MESH)

    def hc(h):
        return pl.ds(h * HD, HD)

    ia = iota((HD, ROWS), 0)
    ii = iota((HD, ROWS), 1)
    for h in range(HEADS):
        a_n[h] = jnp.where(ii == 4 * ia + offs[0, h], 1.0, 0.0).astype(BF)
        fa = ia - 8 * y
        a_f[h] = jnp.where((ii == 64 * fa + offs[1, h]) & (fa >= 0) & (fa < 8), 1.0, 0.0).astype(BF)
        f16[h] = jnp.where((ii[:16] == 64 * ia[:16] + offs[1, h]) & (ia[:16] < 8), 1.0, 0.0).astype(BF)
    for cp in loads[:3]:
        cp.wait()
    pad8 = jnp.zeros((8, HD), F32)
    for h in range(HEADS):
        rows = [nn(f16[h], x[:, hc(h)])[:8] for x in (k, v, q)]
        p1s[h] = low(jnp.concatenate(rows + [pad8], 0))
    for h in range(HEADS):
        nkv[pos, h, 0:128, :] = low(nn(a_n[h], k[:, hc(h)]))
        nkv[pos, h, 128:256, :] = low(nn(a_n[h], v[:, hc(h)]))
    for t in range(1, 4):
        @pl.when((t > pos + 1) | ((t == pos + 1) & (pos > 0)))
        def _():
            nkv[t] = jnp.zeros((HEADS, 256, HD), BF)

    def near_send(base, slot, to):
        return [rc(nkv.at[slot, h], nkv.at[slot, h], base + h, to) for h in range(HEADS)]

    z_even = z % 2 == 0
    near_z = near_send(40, pos, zpart)
    near_x = near_send(44, pos, xpart)
    relay = near_send(48, (pos + 1) % 2, zpart)

    def local_fwd(h):
        for ib in range(2):
            nk = 256 * (ib + 1)
            qs = slice(ib * 256, ib * 256 + 256)
            st = nt(k[0:nk, hc(h)], q[qs, hc(h)]) * SCALE
            jj = iota((nk, 256), 0)
            qq = iota((nk, 256), 1) + ib * 256
            st = jnp.where(jj <= qq, st, NEG)
            mx = jnp.max(st, 0, keepdims=True).astype(BF).astype(F32)
            e = jnp.exp(st - mx)
            el = low(e)
            e_l[h, 0:nk, qs] = el
            o_l[h, :, qs] = tn(v[0:nk, hc(h)], el)
            st_l[h, 0:1, qs] = mx
            st_l[h, 1:2, qs] = jnp.sum(e, 0, keepdims=True)

    local_fwd(0)
    local_fwd(1)
    loads[3].wait()
    pl.semaphore_wait(barrier, len(partners))

    p1 = [rc(p1s.at[yx[n][0]], p1r.at[xh, y], n, dev(yx[n][0], z, yx[n][1])) for n in range(7)]
    for cp in p1:
        cp.start()
    p1r[xh, y] = p1s[y]

    @pl.when(pos != 3)
    def _():
        for cp in near_x:
            cp.start()

    @pl.when(z_even)
    def _():
        for cp in near_z:
            cp.start()

    def pieces(src, dst, base, to, count):
        size = ROWS // count
        return [rc(src.at[pl.ds(size * n, size)], dst.at[pl.ds(size * n, size)], base + n, to)
                for n in range(count)]

    cg_x = pieces(g, gbuf.at[1], 52, across, 4)
    cg_core = rc(g, gbuf.at[0], 28, core)
    cg_f = pieces(gbuf.at[1], gbuf.at[2], 56, core, 4)
    cg_core.start()
    local_fwd(2)
    local_fwd(3)
    for cp in p1:
        cp.wait()
    for hh in range(2):
        got = [p1r[hh, t].astype(F32) for t in range(NY)]
        fkv[z, hh] = low(jnp.concatenate([x[0:8] for x in got] + [x[8:16] for x in got], 0))
    p3 = [rc(fkv.at[z], fkv.at[z], 7 + d, zps[d]) for d in range(7)]
    for d in (3, 2, 4, 1, 5, 0, 6):
        p3[d].start()
    for cp in cg_x:
        cp.start()
    got = [p1r[xh, t].astype(F32) for t in range(NY)]
    fq = low(jnp.concatenate([x[16:24] for x in got] + [jnp.zeros((96, HD), F32)], 0))

    def grad_part(slot, half):
        src = [(l, c), (l, 1 - c), (1 - l, c), (1 - l, 1 - c)][slot]
        cols = pl.ds(pl.multiple_of((src[0] * 2 + src[1]) * ROWS, ROWS), ROWS)
        r = slice(256 * half, 256 * half + 256)
        part = nt(w[:, cols], g[r, :] if slot == 0 else gbuf[slot - 1, r, :])
        if slot:
            part = part + gacc[:, r]
        gacc[:, r] = part

    loads[4].wait()
    for n in range(2):
        grad_part(0, n)
    cg_core.wait()
    for n in range(2):
        grad_part(1, n)

    @pl.when(z_even)
    def _():
        for h in range(HEADS):
            near_x[h].wait_recv()
            relay[h].start()

    def scores(kk, qq, vv, seen):
        st = nt(kk, qq) * SCALE
        st = jnp.where(seen, st, NEG)
        mx = jnp.max(st, 0, keepdims=True).astype(BF).astype(F32)
        e = jnp.exp(st - mx)
        el = low(e)
        hi, lo = hi_lo(jnp.sum(e, 0, keepdims=True))
        return el, low(jnp.concatenate([tn(vv, el), mx, hi, lo, jnp.zeros((13, HD), F32)], 0))

    jn = iota((ROWS, HD), 0)
    an = iota((ROWS, HD), 1)
    near_seen = jn <= pos * 128 + an
    key_index = ((jn // 8) % 4) * 128 + (jn // 64) * 16 + ((jn // 32) % 2) * 8 + jn % 8
    query_index = (an // 8) * 128 + z * 16 + xh * 8 + an % 8
    far_seen = key_index <= query_index

    def near_k(h):
        return nkv[:, h, 0:128, :].reshape(ROWS, HD)

    def near_v(h):
        return nkv[:, h, 128:256, :].reshape(ROWS, HD)

    jt = iota((ROWS, HD), 0)
    at = iota((ROWS, HD), 1)
    for h in range(HEADS):
        back_n[h] = jnp.where(jt == 4 * at + offs[0, h], 1.0, 0.0).astype(BF)
        back_f[h] = jnp.where((jt == 64 * at + offs[1, h]) & (at < 8), 1.0, 0.0).astype(BF)[:, 0:16]

    for cp in p3:
        cp.wait_recv()
    far_k = fkv[:, :, 0:32, :].reshape(ROWS, HD)
    far_v = fkv[:, :, 32:64, :].reshape(ROWS, HD)
    el, block = scores(far_k, fq, far_v, far_seen)
    e_f[...] = el
    fo[y] = block
    p4 = [rc(fo.at[y], fo.at[y], 14 + d, yps[d]) for d in range(3)]
    for cp in p4:
        cp.start()

    for h in range(HEADS):
        @pl.when(z % 2 == 1)
        def _():
            near_z[h].wait_recv()
            relay[h].wait_recv()

        @pl.when(pos == 3)
        def _():
            near_x[h].wait_recv()

        qq = low(nn(a_n[h], q[:, hc(h)]))
        q_n[h] = qq
        el, block = scores(near_k(h), qq, near_v(h), near_seen)
        e_n[h] = el
        o_n[h] = block

    lane = iota((1, ROWS), 1)

    def spread(block, sel):
        both = nn(block, sel)
        return both[0:HD], both[HD:HD + 1], both[HD + 1:HD + 2] + both[HD + 2:HD + 3]

    def picked(cf, inner, sel):
        c_hi, c_lo = hi_lo(cf)
        i_hi, i_lo = hi_lo(inner)
        rows = jnp.concatenate([c_hi, c_lo, i_hi, i_lo, jnp.zeros((12, ROWS), F32)], 0)
        return nt(low(rows), sel)

    def combine(h):
        on, mn, sn = spread(o_n[h], a_n[h])
        of, mf, sf = spread(fo[h], a_f[h])
        mn = jnp.where(lane % 4 == offs[0, h], mn, NEG)
        mf = jnp.where(lane % 64 == offs[1, h], mf, NEG)
        ml = st_l[h, 0:1, :]
        top = jnp.maximum(ml, jnp.maximum(mn, mf))
        wl, wn, wf = jnp.exp(ml - top), jnp.exp(mn - top), jnp.exp(mf - top)
        total = st_l[h, 1:2, :] * wl + sn * wn + sf * wf
        inv = 1.0 / total
        out = low((o_l[h] * wl + on * wn + of * wf) * inv)
        att[hc(h), :] = out
        c_l[h, 0:1, :] = wl * inv
        c_l[h, 1:2, :] = wn * inv
        c_l[h, 2:3, :] = wf * inv

    def row_stats(h):
        inner = jnp.sum(dot_[hc(h), :].astype(F32) * att[hc(h), :].astype(F32), 0, keepdims=True)
        inn[h, 0:1, :] = inner
        far = picked(c_l[h, 2:3, :], inner, a_f[h])
        p5s[h] = low(jnp.concatenate([nn(f16[h], do_[:, hc(h)])[:8], far[:8]], 0))
        c_n[h] = picked(c_l[h, 1:2, :], inner, a_n[h])

    for cp in p4:
        cp.wait()
    for h in range(HEADS):
        combine(h)
    def mixed_part(ll, cc, n):
        cols = pl.ds(pl.multiple_of((ll * 2 + cc) * ROWS, ROWS), ROWS)
        return tn(att[:, 256 * n:256 * n + 256], w[:, cols])

    def half(n):
        return pl.ds(256 * n, 256)

    cm0 = pieces(mcs.at[0], mcr.at[0], 60, core, 2)
    cm1 = pieces(mcs.at[1], mcr.at[1], 62, core, 2)
    cmx = [rc(mxs.at[pl.ds(64 * n, 64)], mxr.at[pl.ds(64 * n, 64)], 64 + n, across) for n in range(8)]

    def send_mixed(n):
        if n >= 2:
            cmx[n - 2].wait_send()
        cmx[n].start()

    for n in range(2):
        mcs[0, half(n), :] = low(mixed_part(1 - l, 1 - c, n))
        cm0[n].start()
    for n in range(2):
        part = mixed_part(1 - l, c, n)
        cm0[n].wait()
        mxs[half(n), :] = low(part + mcr[0, half(n), :].astype(F32))
        send_mixed(n)

    for n in range(2):
        for i in (2 * n, 2 * n + 1):
            cg_x[i].wait_recv()
            cg_f[i].start()
        grad_part(2, n)
    for n in range(2):
        cg_f[2 * n].wait_recv()
        cg_f[2 * n + 1].wait_recv()
        grad_part(3, n)
        r = slice(256 * n, 256 * n + 256)
        dot_[:, r] = low(gacc[:, r])
        do_[r, :] = dot_[:, r].T
    for h in range(HEADS):
        row_stats(h)
    p5 = [rc(p5s.at[ys[d]], p5r.at[y], 17 + d, yps[d]) for d in range(3)]
    for cp in p5:
        cp.start()
    p5r[y] = p5s[y]

    def near_bwd(h):
        dd = low(nn(a_n[h], do_[:, hc(h)]))
        prob = e_n[h].astype(F32) * (c_n[h, 0:1, :] + c_n[h, 1:2, :])
        ds = low(prob * (nt(near_v(h), dd) - (c_n[h, 2:3, :] + c_n[h, 3:4, :])))
        ng[:, h, 0:128, :] = low(nn(ds, q_n[h]) * SCALE).reshape(4, HD, HD)
        ng[:, h, 128:256, :] = low(nn(low(prob), dd)).reshape(4, HD, HD)
        dqt[h] = nn(low(tn(near_k(h), ds) * SCALE), a_n[h])

    def back_copy(slot, into, base, to):
        return [rc(ng.at[slot, h], nrb.at[into, h], base + h, to) for h in range(HEADS)]

    back_z = back_copy(0, 0, 72, zpart)
    back_x = back_copy((pos + 3) % 4, 1, 76, xpart)
    back_rx = back_copy(0, 2, 80, xpart)
    back_rz = back_copy(1, 2, 80, zpart)
    for h in range(HEADS):
        near_bwd(h)

        @pl.when(z % 2 == 1)
        def _():
            back_z[h].start()
            back_x[h].start()

    for cp in p5:
        cp.wait()
    got = [p5r[t].astype(F32) for t in range(NY)]
    fd = low(jnp.concatenate([x[0:8] for x in got] + [jnp.zeros((96, HD), F32)], 0))
    stat = got[0][8:16] + got[1][8:16] + got[2][8:16] + got[3][8:16]
    far_k = fkv[:, :, 0:32, :].reshape(ROWS, HD)
    far_v = fkv[:, :, 32:64, :].reshape(ROWS, HD)
    prob = e_f[...].astype(F32) * (stat[0:1] + stat[1:2])
    ds = low(prob * (nt(far_v, fd) - (stat[2:3] + stat[3:4])))
    fgr[:, :, 0:32, :] = low(nn(ds, fq) * SCALE).reshape(NZ, 2, 32, HD)
    fgr[:, :, 32:64, :] = low(nn(low(prob), fd)).reshape(NZ, 2, 32, HD)
    p6 = [rc(fgr.at[(z + d + 1) % NZ], rz.at[d], 20 + d, zps[d]) for d in range(7)]
    for d in (3, 2, 4, 1, 5, 0, 6):
        p6[d].start()
    fdq = tn(ds, far_k)[0:32] * SCALE

    def local_bwd(h):
        for ib in range(2):
            nk = 256 * (ib + 1)
            qs = slice(ib * 256, ib * 256 + 256)
            prob = e_l[h, 0:nk, qs].astype(F32) * c_l[h, 0:1, qs]
            dp = nn(v[0:nk, hc(h)], dot_[hc(h), qs])
            ds = low(prob * (dp - inn[h, 0:1, qs]))
            vt = nn(low(prob), do_[qs, hc(h)])
            kt = nn(ds, q[qs, hc(h)]) * SCALE
            if ib == 0:
                dva[0:nk, hc(h)] = vt
                dka[0:nk, hc(h)] = kt
            else:
                dva[0:256, hc(h)] = dva[0:256, hc(h)] + vt[0:256]
                dka[0:256, hc(h)] = dka[0:256, hc(h)] + kt[0:256]
                dva[256:512, hc(h)] = vt[256:512]
                dka[256:512, hc(h)] = kt[256:512]
            qt = tn(k[0:nk, hc(h)], ds) * SCALE + dqt[h, :, qs]
            dqa[qs, hc(h)] = qt.T

    def add_block(dst, src):
        dst[...] = low(dst[...].astype(F32) + src[...].astype(F32))

    def relay_back(heads):
        @pl.when(pos == 1)
        def _():
            for h in heads:
                back_z[h].wait_recv()
                add_block(ng.at[0, h], nrb.at[0, h])
                back_rx[h].start()

        @pl.when(pos == 3)
        def _():
            for h in heads:
                back_x[h].wait_recv()
                add_block(ng.at[1, h], nrb.at[1, h])
                back_rz[h].start()

    relay_back((0, 1))
    send_mixed(2)
    local_bwd(0)
    relay_back((2, 3))
    send_mixed(3)
    local_bwd(1)
    send_mixed(4)
    local_bwd(2)
    send_mixed(5)
    for cp in p6:
        cp.wait_recv()
    total = fgr[z].astype(F32)
    for d in range(7):
        total = total + rz[d].astype(F32)
    fgr[z] = low(total)
    for hh in range(2):
        for t in range(NY):
            r = slice(8 * t, 8 * t + 8)
            third = jnp.where(xh == hh, fdq[r], 0.0)
            p8s[hh, t] = low(jnp.concatenate(
                [total[hh, r], total[hh, 32 + 8 * t:40 + 8 * t], third, pad8], 0))
    p8 = [rc(p8s.at[yx[n][1], yx[n][0]], p8r.at[xh, y], 29 + n, dev(yx[n][0], z, yx[n][1])) for n in range(7)]
    for cp in p8:
        cp.start()
    p8r[xh, y] = p8s[xh, y]

    local_bwd(3)
    send_mixed(6)
    for n in range(2):
        mcs[1, half(n), :] = low(mixed_part(l, 1 - c, n))
        cm1[n].start()
    send_mixed(7)
    for n in range(2):
        mkeep[half(n), :] = mixed_part(l, c, n)

    cmx[6].wait_send()
    cmx[7].wait_send()
    for n in range(2):
        cm1[n].wait()
        for i in range(4):
            cmx[4 * n + i].wait_recv()
        mixed[half(n), :] = low(mkeep[half(n), :] + mcr[1, half(n), :].astype(F32) + mxr[half(n), :].astype(F32))

    out_mixed = pltpu.make_async_copy(mixed, mixed_h, outs.at[0])
    out_mixed.start()

    def take(copies, slot, into):
        for cp in copies:
            cp.wait_recv()
        add_block(ng.at[slot], nrb.at[into])

    @pl.when(pos == 0)
    def _():
        take(back_z, 0, 0)
        take(back_rx, 0, 2)

    @pl.when(pos == 1)
    def _():
        take(back_rz, 1, 2)

    @pl.when(pos == 2)
    def _():
        take(back_x, 2, 1)

    for cp in p8:
        cp.wait()
    out_rest = []
    for h in range(HEADS):
        x = p8r[0, h].astype(F32) + p8r[1, h].astype(F32)
        wide = jnp.concatenate([x[0:8], x[8:16], x[16:24]], 1)
        far = nn(back_f[h], low(jnp.concatenate([wide, jnp.zeros((8, 3 * HD), F32)], 0)))
        dk[:, hc(h)] = low(dka[:, hc(h)] + nn(back_n[h], ng[pos, h, 0:128, :]) + far[:, 0:HD])
        dv[:, hc(h)] = low(dva[:, hc(h)] + nn(back_n[h], ng[pos, h, 128:256, :]) + far[:, HD:2 * HD])
        dq[:, hc(h)] = low(dqa[:, hc(h)] + far[:, 2 * HD:])
        for n, (a, b) in enumerate([(dk, dk_h), (dv, dv_h), (dq, dq_h)]):
            cp = pltpu.make_async_copy(a.at[:, hc(h)], b.at[:, hc(h)], outs.at[1 + 3 * h + n])
            cp.start()
            out_rest.append(cp)

    for cp in p3 + p6 + cg_x + cg_f:
        cp.wait_send()

    @pl.when(pos != 3)
    def _():
        for cp in near_x:
            cp.wait_send()

    @pl.when(z_even)
    def _():
        for cp in near_z + relay:
            cp.wait_send()

    @pl.when(pos == 1)
    def _():
        for cp in back_rx:
            cp.wait_send()

    @pl.when(pos == 3)
    def _():
        for cp in back_rz:
            cp.wait_send()

    @pl.when(z % 2 == 1)
    def _():
        for cp in back_x + back_z:
            cp.wait_send()
    for cp in [out_mixed] + out_rest:
        cp.wait()


def hand_on(a, b, c, d, a2, b2, c2, d2, hold, in_sem, out_sem):
    pairs = [(a, a2), (b, b2), (c, c2), (d, d2)]
    ins = [pltpu.make_async_copy(x, hold.at[j], in_sem.at[j]) for j, (x, _) in enumerate(pairs)]
    outs = [pltpu.make_async_copy(hold.at[j], x, out_sem.at[j]) for j, (_, x) in enumerate(pairs)]
    for cp in ins:
        cp.start()
    for i, o in zip(ins, outs):
        i.wait()
        o.start()
    for cp in outs:
        cp.wait()


def local(queries, key_rows, value_rows, out_weight, grad_out, offsets):
    hbm = pl.BlockSpec(memory_space=pl.ANY)
    shape = jax.ShapeDtypeStruct((ROWS, ROWS), BF)
    V = pltpu.VMEM
    dma = pltpu.SemaphoreType.DMA
    wide = (ROWS, ROWS)
    outs = pl.pallas_call(
        kernel,
        out_shape=(shape,) * 4,
        in_specs=[pl.BlockSpec(memory_space=pltpu.SMEM)] + [hbm] * 5,
        out_specs=(hbm,) * 4,
        scratch_shapes=[
            V(wide, BF), V(wide, BF), V(wide, BF), V(wide, BF),
            V(wide, BF), V(wide, BF), V(wide, BF), V((ROWS, 4 * ROWS), BF), V(wide, BF),
            V((3, ROWS, ROWS), BF), V(wide, F32), V(wide, BF), V(wide, BF),
            V((4, HEADS, 256, HD), BF),
            V((HEADS, ROWS, ROWS), BF), V((HEADS, ROWS, HD), BF), V((ROWS, HD), BF),
            V((HEADS, HD, ROWS), F32), V((HEADS, 144, HD), BF),
            V((HEADS, 8, ROWS), F32), V((HEADS, 8, HD), F32),
            V((HEADS, HD, HD), BF),
            V((HEADS, HD, ROWS), BF), V((HEADS, HD, ROWS), BF), V((HEADS, 16, ROWS), BF),
            V(wide, BF),
            V((HEADS, 8, ROWS), F32), V((HEADS, 16, HD), F32), V((HEADS, 8, ROWS), F32),
            V((HEADS, HD, ROWS), F32), V(wide, F32), V(wide, F32), V(wide, F32),
            V((NY, 32, HD), BF), V((2, NY, 32, HD), BF), V((NZ, 2, 64, HD), BF), V((NY, 144, HD), BF),
            V((NY, 16, HD), BF), V((NY, 16, HD), BF), V((NZ, 2, 64, HD), BF), V((NZ - 1, 2, 64, HD), BF),
            V((2, NY, 32, HD), BF), V((2, NY, 32, HD), BF),
            V((4, HEADS, 256, HD), BF), V((3, HEADS, 256, HD), BF),
            V((2, ROWS, ROWS), BF), V((2, ROWS, ROWS), BF), V(wide, F32),
            V(wide, BF), V(wide, BF),
            V((HEADS, ROWS, HD), BF), V((HEADS, ROWS, 16), BF),
            dma((5,)), dma((13,)), dma((84,)), dma((84,)),
        ],
        compiler_params=pltpu.CompilerParams(
            collective_id=0, has_side_effects=True, vmem_limit_bytes=56 << 20),
        cost_estimate=pl.CostEstimate(flops=4_400_000_000, bytes_accessed=8 << 20, transcendentals=1_400_000),
        name="dilated",
    )(offsets, queries, key_rows, value_rows, out_weight, grad_out)
    return pl.pallas_call(
        hand_on,
        out_shape=(shape,) * 4,
        in_specs=[hbm] * 4,
        out_specs=(hbm,) * 4,
        scratch_shapes=[V((4, ROWS, ROWS), BF), dma((4,)), dma((4,))],
        name="hand_on",
    )(*outs)


def solution(mesh):
    return jax.shard_map(
        local,
        mesh=mesh,
        in_specs=(
            P("seq", "mp"),
            P("seq", "mp"),
            P("seq", "mp"),
            P("mp", None),
            P("seq", "mp"),
            P(None, "mp"),
        ),
        out_specs=(P("seq", "mp"), P("seq", "mp"), P("seq", "mp"), P("seq", "mp")),
        check_vma=False,
    )
```

```python
import functools

import jax
import jax.numpy as jnp
from jax import lax
from jax.experimental import pallas as pl
from jax.experimental.pallas import tpu as pltpu
from jax.sharding import PartitionSpec as P

MESH = pl.DeviceIdType.MESH
BF = jnp.bfloat16
F32 = jnp.float32
HD = 128
HEADS = 4
ROWS = 512
SCALE = HD ** (-0.5)
NY, NZ = 4, 8
NEG = -1e30


def nn(a, b):
    return lax.dot_general(a, b, (((1,), (0,)), ((), ())), preferred_element_type=F32)


def nt(a, b):
    return lax.dot_general(a, b, (((1,), (1,)), ((), ())), preferred_element_type=F32)


def tn(a, b):
    return lax.dot_general(a, b, (((0,), (0,)), ((), ())), preferred_element_type=F32)


def iota(shape, dim):
    return lax.broadcasted_iota(jnp.int32, shape, dim)


def low(x):
    return x.astype(BF)


def hi_lo(x):
    hi = x.astype(BF).astype(F32)
    return hi, x - hi


def kernel(offs, qh, kh, vh, wh, gh, mixed_h, dq_h, dk_h, dv_h, mixed, dq, dk, dv,
           q, k, v, w, g, gbuf, gacc, dot_, do_, nkv, e_l, e_n, e_f, o_l, o_n,
           st_l, st_n, q_n, a_n, a_f, f16, att, c_l, c_n, inn, dqt, dqa, dka, dva,
           p1s, p1r, fkv, fo, p5s, p5r, fgr, rz, p8s, p8r,
           ng, nrb, mcs, mcr, mkeep, mxs, mxr,
           back_n, back_f, ins, outs, ss, rs):
    s = lax.axis_index("seq")
    m = lax.axis_index("mp")
    y, z, xh = s // 16, (s // 2) % NZ, s % 2
    l, c = m // 2, m % 2
    pos = s % 4

    def dev(yy, zz, hh):
        return ((yy * NZ + zz) * 2 + hh, m)

    core = (s, l * 2 + 1 - c)
    across = (s, (1 - l) * 2 + c)
    xpart = dev(y, z, 1 - xh)
    zpart = dev(y, z + 1 - 2 * (z % 2), xh)
    ys = [(y + d) % NY for d in range(1, NY)]
    yps = [dev(yy, z, xh) for yy in ys]
    zps = [dev(y, (z + d) % NZ, xh) for d in range(1, NZ)]
    yx = [((y + n // 2) % NY, (xh + n % 2) % 2) for n in range(1, 2 * NY)]
    partners = [core, across] + [dev(yy, z, hh) for yy, hh in yx] + zps

    barrier = pltpu.get_barrier_semaphore()
    for p in partners:
        pl.semaphore_signal(barrier, inc=1, device_id=p, device_id_type=MESH)
    loads = [pltpu.make_async_copy(a, b, ins.at[i])
             for i, (a, b) in enumerate([(kh, k), (vh, v), (qh, q), (gh, g), (wh, w)])]
    for cp in loads:
        cp.start()

    def rc(src, dst, i, to):
        return pltpu.make_async_remote_copy(
            src_ref=src, dst_ref=dst, send_sem=ss.at[i], recv_sem=rs.at[i],
            device_id=to, device_id_type=MESH)

    def hc(h):
        return pl.ds(h * HD, HD)

    ia = iota((HD, ROWS), 0)
    ii = iota((HD, ROWS), 1)
    for h in range(HEADS):
        a_n[h] = jnp.where(ii == 4 * ia + offs[0, h], 1.0, 0.0).astype(BF)
        fa = ia - 8 * y
        a_f[h] = jnp.where((ii == 64 * fa + offs[1, h]) & (fa >= 0) & (fa < 8), 1.0, 0.0).astype(BF)
        f16[h] = jnp.where((ii[:16] == 64 * ia[:16] + offs[1, h]) & (ia[:16] < 8), 1.0, 0.0).astype(BF)
    for cp in loads[:3]:
        cp.wait()
    pad8 = jnp.zeros((8, HD), F32)
    for h in range(HEADS):
        rows = [nn(f16[h], x[:, hc(h)])[:8] for x in (k, v, q)]
        p1s[h] = low(jnp.concatenate(rows + [pad8], 0))
    for h in range(HEADS):
        nkv[pos, h, 0:128, :] = low(nn(a_n[h], k[:, hc(h)]))
        nkv[pos, h, 128:256, :] = low(nn(a_n[h], v[:, hc(h)]))
    for t in range(1, 4):
        @pl.when((t > pos + 1) | ((t == pos + 1) & (pos > 0)))
        def _():
            nkv[t] = jnp.zeros((HEADS, 256, HD), BF)

    def near_send(base, slot, to):
        return [rc(nkv.at[slot, h], nkv.at[slot, h], base + h, to) for h in range(HEADS)]

    z_even = z % 2 == 0
    near_z = near_send(40, pos, zpart)
    near_x = near_send(44, pos, xpart)
    relay = near_send(48, (pos + 1) % 2, zpart)

    def local_fwd(h):
        for ib in range(2):
            nk = 256 * (ib + 1)
            qs = slice(ib * 256, ib * 256 + 256)
            st = nt(k[0:nk, hc(h)], q[qs, hc(h)]) * SCALE
            jj = iota((nk, 256), 0)
            qq = iota((nk, 256), 1) + ib * 256
            st = jnp.where(jj <= qq, st, NEG)
            mx = jnp.max(st, 0, keepdims=True).astype(BF).astype(F32)
            e = jnp.exp(st - mx)
            el = low(e)
            e_l[h, 0:nk, qs] = el
            o_l[h, :, qs] = tn(v[0:nk, hc(h)], el)
            st_l[h, 0:1, qs] = mx
            st_l[h, 1:2, qs] = jnp.sum(e, 0, keepdims=True)

    local_fwd(0)
    local_fwd(1)
    loads[3].wait()
    pl.semaphore_wait(barrier, len(partners))

    p1 = [rc(p1s.at[yx[n][0]], p1r.at[xh, y], n, dev(yx[n][0], z, yx[n][1])) for n in range(7)]
    for cp in p1:
        cp.start()
    p1r[xh, y] = p1s[y]

    @pl.when(pos != 3)
    def _():
        for cp in near_x:
            cp.start()

    @pl.when(z_even)
    def _():
        for cp in near_z:
            cp.start()

    def pieces(src, dst, base, to, count):
        size = ROWS // count
        return [rc(src.at[pl.ds(size * n, size)], dst.at[pl.ds(size * n, size)], base + n, to)
                for n in range(count)]

    cg_x = pieces(g, gbuf.at[1], 52, across, 4)
    cg_core = rc(g, gbuf.at[0], 28, core)
    cg_f = pieces(gbuf.at[1], gbuf.at[2], 56, core, 4)
    cg_core.start()
    local_fwd(2)
    local_fwd(3)
    for cp in p1:
        cp.wait()
    for hh in range(2):
        got = [p1r[hh, t].astype(F32) for t in range(NY)]
        fkv[z, hh] = low(jnp.concatenate([x[0:8] for x in got] + [x[8:16] for x in got], 0))
    p3 = [rc(fkv.at[z], fkv.at[z], 7 + d, zps[d]) for d in range(7)]
    for d in (3, 2, 4, 1, 5, 0, 6):
        p3[d].start()
    for cp in cg_x:
        cp.start()
    got = [p1r[xh, t].astype(F32) for t in range(NY)]
    fq = low(jnp.concatenate([x[16:24] for x in got] + [jnp.zeros((96, HD), F32)], 0))

    def grad_part(slot, half):
        src = [(l, c), (l, 1 - c), (1 - l, c), (1 - l, 1 - c)][slot]
        cols = pl.ds(pl.multiple_of((src[0] * 2 + src[1]) * ROWS, ROWS), ROWS)
        r = slice(256 * half, 256 * half + 256)
        part = nt(w[:, cols], g[r, :] if slot == 0 else gbuf[slot - 1, r, :])
        if slot:
            part = part + gacc[:, r]
        gacc[:, r] = part

    loads[4].wait()
    for n in range(2):
        grad_part(0, n)
    cg_core.wait()
    for n in range(2):
        grad_part(1, n)

    @pl.when(z_even)
    def _():
        for h in range(HEADS):
            near_x[h].wait_recv()
            relay[h].start()

    def scores(kk, qq, vv, seen):
        st = nt(kk, qq) * SCALE
        st = jnp.where(seen, st, NEG)
        mx = jnp.max(st, 0, keepdims=True).astype(BF).astype(F32)
        e = jnp.exp(st - mx)
        el = low(e)
        hi, lo = hi_lo(jnp.sum(e, 0, keepdims=True))
        return el, low(jnp.concatenate([tn(vv, el), mx, hi, lo, jnp.zeros((13, HD), F32)], 0))

    jn = iota((ROWS, HD), 0)
    an = iota((ROWS, HD), 1)
    near_seen = jn <= pos * 128 + an
    key_index = ((jn // 8) % 4) * 128 + (jn // 64) * 16 + ((jn // 32) % 2) * 8 + jn % 8
    query_index = (an // 8) * 128 + z * 16 + xh * 8 + an % 8
    far_seen = key_index <= query_index

    def near_k(h):
        return nkv[:, h, 0:128, :].reshape(ROWS, HD)

    def near_v(h):
        return nkv[:, h, 128:256, :].reshape(ROWS, HD)

    jt = iota((ROWS, HD), 0)
    at = iota((ROWS, HD), 1)
    for h in range(HEADS):
        back_n[h] = jnp.where(jt == 4 * at + offs[0, h], 1.0, 0.0).astype(BF)
        back_f[h] = jnp.where((jt == 64 * at + offs[1, h]) & (at < 8), 1.0, 0.0).astype(BF)[:, 0:16]

    for cp in p3:
        cp.wait_recv()
    far_k = fkv[:, :, 0:32, :].reshape(ROWS, HD)
    far_v = fkv[:, :, 32:64, :].reshape(ROWS, HD)
    el, block = scores(far_k, fq, far_v, far_seen)
    e_f[...] = el
    fo[y] = block
    p4 = [rc(fo.at[y], fo.at[y], 14 + d, yps[d]) for d in range(3)]
    for cp in p4:
        cp.start()

    for h in range(HEADS):
        @pl.when(z % 2 == 1)
        def _():
            near_z[h].wait_recv()
            relay[h].wait_recv()

        @pl.when(pos == 3)
        def _():
            near_x[h].wait_recv()

        qq = low(nn(a_n[h], q[:, hc(h)]))
        q_n[h] = qq
        el, block = scores(near_k(h), qq, near_v(h), near_seen)
        e_n[h] = el
        o_n[h] = block

    lane = iota((1, ROWS), 1)

    def spread(block, sel):
        both = nn(block, sel)
        return both[0:HD], both[HD:HD + 1], both[HD + 1:HD + 2] + both[HD + 2:HD + 3]

    def picked(cf, inner, sel):
        c_hi, c_lo = hi_lo(cf)
        i_hi, i_lo = hi_lo(inner)
        rows = jnp.concatenate([c_hi, c_lo, i_hi, i_lo, jnp.zeros((12, ROWS), F32)], 0)
        return nt(low(rows), sel)

    def combine(h):
        on, mn, sn = spread(o_n[h], a_n[h])
        of, mf, sf = spread(fo[h], a_f[h])
        mn = jnp.where(lane % 4 == offs[0, h], mn, NEG)
        mf = jnp.where(lane % 64 == offs[1, h], mf, NEG)
        ml = st_l[h, 0:1, :]
        top = jnp.maximum(ml, jnp.maximum(mn, mf))
        wl, wn, wf = jnp.exp(ml - top), jnp.exp(mn - top), jnp.exp(mf - top)
        total = st_l[h, 1:2, :] * wl + sn * wn + sf * wf
        inv = 1.0 / total
        out = low((o_l[h] * wl + on * wn + of * wf) * inv)
        att[hc(h), :] = out
        c_l[h, 0:1, :] = wl * inv
        c_l[h, 1:2, :] = wn * inv
        c_l[h, 2:3, :] = wf * inv

    def row_stats(h):
        inner = jnp.sum(dot_[hc(h), :].astype(F32) * att[hc(h), :].astype(F32), 0, keepdims=True)
        inn[h, 0:1, :] = inner
        far = picked(c_l[h, 2:3, :], inner, a_f[h])
        p5s[h] = low(jnp.concatenate([nn(f16[h], do_[:, hc(h)])[:8], far[:8]], 0))
        c_n[h] = picked(c_l[h, 1:2, :], inner, a_n[h])

    for cp in p4:
        cp.wait()
    for h in range(HEADS):
        combine(h)
    def mixed_part(ll, cc, n):
        cols = pl.ds(pl.multiple_of((ll * 2 + cc) * ROWS, ROWS), ROWS)
        return tn(att[:, 256 * n:256 * n + 256], w[:, cols])

    def half(n):
        return pl.ds(256 * n, 256)

    cm0 = pieces(mcs.at[0], mcr.at[0], 60, core, 2)
    cm1 = pieces(mcs.at[1], mcr.at[1], 62, core, 2)
    cmx = [rc(mxs.at[pl.ds(64 * n, 64)], mxr.at[pl.ds(64 * n, 64)], 64 + n, across) for n in range(8)]

    def send_mixed(n):
        if n >= 4:
            cmx[n - 4].wait_send()
        cmx[n].start()

    for n in range(2):
        mcs[0, half(n), :] = low(mixed_part(1 - l, 1 - c, n))
        cm0[n].start()
    for n in range(2):
        part = mixed_part(1 - l, c, n)
        cm0[n].wait()
        mxs[half(n), :] = low(part + mcr[0, half(n), :].astype(F32))
        send_mixed(2 * n)
        send_mixed(2 * n + 1)

    for n in range(2):
        for i in (2 * n, 2 * n + 1):
            cg_x[i].wait_recv()
            cg_f[i].start()
        grad_part(2, n)
    for n in range(2):
        cg_f[2 * n].wait_recv()
        cg_f[2 * n + 1].wait_recv()
        grad_part(3, n)
        r = slice(256 * n, 256 * n + 256)
        dot_[:, r] = low(gacc[:, r])
        do_[r, :] = dot_[:, r].T
    for h in range(HEADS):
        row_stats(h)
    p5 = [rc(p5s.at[ys[d]], p5r.at[y], 17 + d, yps[d]) for d in range(3)]
    for cp in p5:
        cp.start()
    p5r[y] = p5s[y]

    def near_bwd(h):
        dd = low(nn(a_n[h], do_[:, hc(h)]))
        prob = e_n[h].astype(F32) * (c_n[h, 0:1, :] + c_n[h, 1:2, :])
        ds = low(prob * (nt(near_v(h), dd) - (c_n[h, 2:3, :] + c_n[h, 3:4, :])))
        ng[:, h, 0:128, :] = low(nn(ds, q_n[h]) * SCALE).reshape(4, HD, HD)
        ng[:, h, 128:256, :] = low(nn(low(prob), dd)).reshape(4, HD, HD)
        dqt[h] = nn(low(tn(near_k(h), ds) * SCALE), a_n[h])

    def back_copy(slot, into, base, to):
        return [rc(ng.at[slot, h], nrb.at[into, h], base + h, to) for h in range(HEADS)]

    back_z = back_copy(0, 0, 72, zpart)
    back_x = back_copy((pos + 3) % 4, 1, 76, xpart)
    back_rx = back_copy(0, 2, 80, xpart)
    back_rz = back_copy(1, 2, 80, zpart)
    for h in range(HEADS):
        near_bwd(h)

        @pl.when(z % 2 == 1)
        def _():
            back_z[h].start()
            back_x[h].start()

    for cp in p5:
        cp.wait()
    got = [p5r[t].astype(F32) for t in range(NY)]
    fd = low(jnp.concatenate([x[0:8] for x in got] + [jnp.zeros((96, HD), F32)], 0))
    stat = got[0][8:16] + got[1][8:16] + got[2][8:16] + got[3][8:16]
    far_k = fkv[:, :, 0:32, :].reshape(ROWS, HD)
    far_v = fkv[:, :, 32:64, :].reshape(ROWS, HD)
    prob = e_f[...].astype(F32) * (stat[0:1] + stat[1:2])
    ds = low(prob * (nt(far_v, fd) - (stat[2:3] + stat[3:4])))
    fgr[:, :, 0:32, :] = low(nn(ds, fq) * SCALE).reshape(NZ, 2, 32, HD)
    fgr[:, :, 32:64, :] = low(nn(low(prob), fd)).reshape(NZ, 2, 32, HD)
    p6 = [rc(fgr.at[(z + d + 1) % NZ], rz.at[d], 20 + d, zps[d]) for d in range(7)]
    for d in (3, 2, 4, 1, 5, 0, 6):
        p6[d].start()
    fdq = tn(ds, far_k)[0:32] * SCALE

    def local_bwd(h):
        for ib in range(2):
            nk = 256 * (ib + 1)
            qs = slice(ib * 256, ib * 256 + 256)
            prob = e_l[h, 0:nk, qs].astype(F32) * c_l[h, 0:1, qs]
            dp = nn(v[0:nk, hc(h)], dot_[hc(h), qs])
            ds = low(prob * (dp - inn[h, 0:1, qs]))
            vt = nn(low(prob), do_[qs, hc(h)])
            kt = nn(ds, q[qs, hc(h)]) * SCALE
            if ib == 0:
                dva[0:nk, hc(h)] = vt
                dka[0:nk, hc(h)] = kt
            else:
                dva[0:256, hc(h)] = dva[0:256, hc(h)] + vt[0:256]
                dka[0:256, hc(h)] = dka[0:256, hc(h)] + kt[0:256]
                dva[256:512, hc(h)] = vt[256:512]
                dka[256:512, hc(h)] = kt[256:512]
            qt = tn(k[0:nk, hc(h)], ds) * SCALE + dqt[h, :, qs]
            dqa[qs, hc(h)] = qt.T

    def add_block(dst, src):
        dst[...] = low(dst[...].astype(F32) + src[...].astype(F32))

    def relay_back(heads):
        @pl.when(pos == 1)
        def _():
            for h in heads:
                back_z[h].wait_recv()
                add_block(ng.at[0, h], nrb.at[0, h])
                back_rx[h].start()

        @pl.when(pos == 3)
        def _():
            for h in heads:
                back_x[h].wait_recv()
                add_block(ng.at[1, h], nrb.at[1, h])
                back_rz[h].start()

    relay_back((0, 1))
    local_bwd(0)
    relay_back((2, 3))
    send_mixed(4)
    local_bwd(1)
    send_mixed(5)
    local_bwd(2)
    for cp in p6:
        cp.wait_recv()
    total = fgr[z].astype(F32)
    for d in range(7):
        total = total + rz[d].astype(F32)
    fgr[z] = low(total)
    for hh in range(2):
        for t in range(NY):
            r = slice(8 * t, 8 * t + 8)
            third = jnp.where(xh == hh, fdq[r], 0.0)
            p8s[hh, t] = low(jnp.concatenate(
                [total[hh, r], total[hh, 32 + 8 * t:40 + 8 * t], third, pad8], 0))
    p8 = [rc(p8s.at[yx[n][1], yx[n][0]], p8r.at[xh, y], 29 + n, dev(yx[n][0], z, yx[n][1])) for n in range(7)]
    for cp in p8:
        cp.start()
    p8r[xh, y] = p8s[xh, y]

    local_bwd(3)
    send_mixed(6)
    for n in range(2):
        mcs[1, half(n), :] = low(mixed_part(l, 1 - c, n))
        cm1[n].start()
    send_mixed(7)
    for n in range(2):
        mkeep[half(n), :] = mixed_part(l, c, n)

    for n in range(4, 8):
        cmx[n].wait_send()
    for n in range(2):
        cm1[n].wait()
        for i in range(4):
            cmx[4 * n + i].wait_recv()
        mixed[half(n), :] = low(mkeep[half(n), :] + mcr[1, half(n), :].astype(F32) + mxr[half(n), :].astype(F32))

    out_mixed = pltpu.make_async_copy(mixed, mixed_h, outs.at[0])
    out_mixed.start()

    def take(copies, slot, into):
        for cp in copies:
            cp.wait_recv()
        add_block(ng.at[slot], nrb.at[into])

    @pl.when(pos == 0)
    def _():
        take(back_z, 0, 0)
        take(back_rx, 0, 2)

    @pl.when(pos == 1)
    def _():
        take(back_rz, 1, 2)

    @pl.when(pos == 2)
    def _():
        take(back_x, 2, 1)

    for cp in p8:
        cp.wait()
    out_rest = []
    for h in range(HEADS):
        x = p8r[0, h].astype(F32) + p8r[1, h].astype(F32)
        wide = jnp.concatenate([x[0:8], x[8:16], x[16:24]], 1)
        far = nn(back_f[h], low(jnp.concatenate([wide, jnp.zeros((8, 3 * HD), F32)], 0)))
        dk[:, hc(h)] = low(dka[:, hc(h)] + nn(back_n[h], ng[pos, h, 0:128, :]) + far[:, 0:HD])
        dv[:, hc(h)] = low(dva[:, hc(h)] + nn(back_n[h], ng[pos, h, 128:256, :]) + far[:, HD:2 * HD])
        dq[:, hc(h)] = low(dqa[:, hc(h)] + far[:, 2 * HD:])
        for n, (a, b) in enumerate([(dk, dk_h), (dv, dv_h), (dq, dq_h)]):
            cp = pltpu.make_async_copy(a.at[:, hc(h)], b.at[:, hc(h)], outs.at[1 + 3 * h + n])
            cp.start()
            out_rest.append(cp)

    for cp in p3 + p6 + cg_x + cg_f:
        cp.wait_send()

    @pl.when(pos != 3)
    def _():
        for cp in near_x:
            cp.wait_send()

    @pl.when(z_even)
    def _():
        for cp in near_z + relay:
            cp.wait_send()

    @pl.when(pos == 1)
    def _():
        for cp in back_rx:
            cp.wait_send()

    @pl.when(pos == 3)
    def _():
        for cp in back_rz:
            cp.wait_send()

    @pl.when(z % 2 == 1)
    def _():
        for cp in back_x + back_z:
            cp.wait_send()
    for cp in [out_mixed] + out_rest:
        cp.wait()


def hand_on(a, b, c, d, a2, b2, c2, d2, hold, in_sem, out_sem):
    pairs = [(a, a2), (b, b2), (c, c2), (d, d2)]
    ins = [pltpu.make_async_copy(x, hold.at[j], in_sem.at[j]) for j, (x, _) in enumerate(pairs)]
    outs = [pltpu.make_async_copy(hold.at[j], x, out_sem.at[j]) for j, (_, x) in enumerate(pairs)]
    for cp in ins:
        cp.start()
    for i, o in zip(ins, outs):
        i.wait()
        o.start()
    for cp in outs:
        cp.wait()


def local(queries, key_rows, value_rows, out_weight, grad_out, offsets):
    hbm = pl.BlockSpec(memory_space=pl.ANY)
    shape = jax.ShapeDtypeStruct((ROWS, ROWS), BF)
    V = pltpu.VMEM
    dma = pltpu.SemaphoreType.DMA
    wide = (ROWS, ROWS)
    outs = pl.pallas_call(
        kernel,
        out_shape=(shape,) * 4,
        in_specs=[pl.BlockSpec(memory_space=pltpu.SMEM)] + [hbm] * 5,
        out_specs=(hbm,) * 4,
        scratch_shapes=[
            V(wide, BF), V(wide, BF), V(wide, BF), V(wide, BF),
            V(wide, BF), V(wide, BF), V(wide, BF), V((ROWS, 4 * ROWS), BF), V(wide, BF),
            V((3, ROWS, ROWS), BF), V(wide, F32), V(wide, BF), V(wide, BF),
            V((4, HEADS, 256, HD), BF),
            V((HEADS, ROWS, ROWS), BF), V((HEADS, ROWS, HD), BF), V((ROWS, HD), BF),
            V((HEADS, HD, ROWS), F32), V((HEADS, 144, HD), BF),
            V((HEADS, 8, ROWS), F32), V((HEADS, 8, HD), F32),
            V((HEADS, HD, HD), BF),
            V((HEADS, HD, ROWS), BF), V((HEADS, HD, ROWS), BF), V((HEADS, 16, ROWS), BF),
            V(wide, BF),
            V((HEADS, 8, ROWS), F32), V((HEADS, 16, HD), F32), V((HEADS, 8, ROWS), F32),
            V((HEADS, HD, ROWS), F32), V(wide, F32), V(wide, F32), V(wide, F32),
            V((NY, 32, HD), BF), V((2, NY, 32, HD), BF), V((NZ, 2, 64, HD), BF), V((NY, 144, HD), BF),
            V((NY, 16, HD), BF), V((NY, 16, HD), BF), V((NZ, 2, 64, HD), BF), V((NZ - 1, 2, 64, HD), BF),
            V((2, NY, 32, HD), BF), V((2, NY, 32, HD), BF),
            V((4, HEADS, 256, HD), BF), V((3, HEADS, 256, HD), BF),
            V((2, ROWS, ROWS), BF), V((2, ROWS, ROWS), BF), V(wide, F32),
            V(wide, BF), V(wide, BF),
            V((HEADS, ROWS, HD), BF), V((HEADS, ROWS, 16), BF),
            dma((5,)), dma((13,)), dma((84,)), dma((84,)),
        ],
        compiler_params=pltpu.CompilerParams(
            collective_id=0, has_side_effects=True, vmem_limit_bytes=56 << 20),
        cost_estimate=pl.CostEstimate(flops=4_400_000_000, bytes_accessed=8 << 20, transcendentals=1_400_000),
        name="dilated",
    )(offsets, queries, key_rows, value_rows, out_weight, grad_out)
    return pl.pallas_call(
        hand_on,
        out_shape=(shape,) * 4,
        in_specs=[hbm] * 4,
        out_specs=(hbm,) * 4,
        scratch_shapes=[V((4, ROWS, ROWS), BF), dma((4,)), dma((4,))],
        name="hand_on",
    )(*outs)


def solution(mesh):
    return jax.shard_map(
        local,
        mesh=mesh,
        in_specs=(
            P("seq", "mp"),
            P("seq", "mp"),
            P("seq", "mp"),
            P("mp", None),
            P("seq", "mp"),
            P(None, "mp"),
        ),
        out_specs=(P("seq", "mp"), P("seq", "mp"), P("seq", "mp"), P("seq", "mp")),
        check_vma=False,
    )
```

```python
import functools

import jax
import jax.numpy as jnp
from jax import lax
from jax.experimental import pallas as pl
from jax.experimental.pallas import tpu as pltpu
from jax.sharding import PartitionSpec as P

MESH = pl.DeviceIdType.MESH
BF = jnp.bfloat16
F32 = jnp.float32
HD = 128
HEADS = 4
ROWS = 512
SCALE = HD ** (-0.5)
NY, NZ = 4, 8
NEG = -1e30


def nn(a, b):
    return lax.dot_general(a, b, (((1,), (0,)), ((), ())), preferred_element_type=F32)


def nt(a, b):
    return lax.dot_general(a, b, (((1,), (1,)), ((), ())), preferred_element_type=F32)


def tn(a, b):
    return lax.dot_general(a, b, (((0,), (0,)), ((), ())), preferred_element_type=F32)


def iota(shape, dim):
    return lax.broadcasted_iota(jnp.int32, shape, dim)


def low(x):
    return x.astype(BF)


def hi_lo(x):
    hi = x.astype(BF).astype(F32)
    return hi, x - hi


def kernel(offs, qh, kh, vh, wh, gh, mixed_h, dq_h, dk_h, dv_h, mixed, dq, dk, dv,
           q, k, v, w, g, gbuf, gacc, dot_, do_, nkv, e_l, e_n, e_f, o_l, o_n,
           st_l, st_n, q_n, a_n, a_f, f16, att, c_l, c_n, inn, dqt, dqa, dka, dva,
           p1s, p1r, fkv, fo, p5s, p5r, fgr, rz, p8s, p8r,
           ng, nrb, mcs, mcr, mkeep, mxs, mxr,
           back_n, back_f, att_t, ins, outs, ss, rs):
    s = lax.axis_index("seq")
    m = lax.axis_index("mp")
    y, z, xh = s // 16, (s // 2) % NZ, s % 2
    l, c = m // 2, m % 2
    pos = s % 4

    def dev(yy, zz, hh):
        return ((yy * NZ + zz) * 2 + hh, m)

    core = (s, l * 2 + 1 - c)
    across = (s, (1 - l) * 2 + c)
    xpart = dev(y, z, 1 - xh)
    zpart = dev(y, z + 1 - 2 * (z % 2), xh)
    ys = [(y + d) % NY for d in range(1, NY)]
    yps = [dev(yy, z, xh) for yy in ys]
    zps = [dev(y, (z + d) % NZ, xh) for d in range(1, NZ)]
    yx = [((y + n // 2) % NY, (xh + n % 2) % 2) for n in range(1, 2 * NY)]
    partners = [core, across] + [dev(yy, z, hh) for yy, hh in yx] + zps

    barrier = pltpu.get_barrier_semaphore()
    for p in partners:
        pl.semaphore_signal(barrier, inc=1, device_id=p, device_id_type=MESH)
    loads = [pltpu.make_async_copy(a, b, ins.at[i])
             for i, (a, b) in enumerate([(kh, k), (vh, v), (qh, q), (gh, g), (wh, w)])]
    for cp in loads:
        cp.start()

    def rc(src, dst, i, to):
        return pltpu.make_async_remote_copy(
            src_ref=src, dst_ref=dst, send_sem=ss.at[i], recv_sem=rs.at[i],
            device_id=to, device_id_type=MESH)

    def hc(h):
        return pl.ds(h * HD, HD)

    ia = iota((HD, ROWS), 0)
    ii = iota((HD, ROWS), 1)
    for h in range(HEADS):
        a_n[h] = jnp.where(ii == 4 * ia + offs[0, h], 1.0, 0.0).astype(BF)
        fa = ia - 8 * y
        a_f[h] = jnp.where((ii == 64 * fa + offs[1, h]) & (fa >= 0) & (fa < 8), 1.0, 0.0).astype(BF)
        f16[h] = jnp.where((ii[:16] == 64 * ia[:16] + offs[1, h]) & (ia[:16] < 8), 1.0, 0.0).astype(BF)
    for cp in loads[:3]:
        cp.wait()
    pad8 = jnp.zeros((8, HD), F32)
    for h in range(HEADS):
        rows = [nn(f16[h], x[:, hc(h)])[:8] for x in (k, v, q)]
        p1s[h] = low(jnp.concatenate(rows + [pad8], 0))
    for h in range(HEADS):
        nkv[pos, h, 0:128, :] = low(nn(a_n[h], k[:, hc(h)]))
        nkv[pos, h, 128:256, :] = low(nn(a_n[h], v[:, hc(h)]))
    for t in range(1, 4):
        @pl.when((t > pos + 1) | ((t == pos + 1) & (pos > 0)))
        def _():
            nkv[t] = jnp.zeros((HEADS, 256, HD), BF)

    def near_send(base, slot, to):
        return [rc(nkv.at[slot, h], nkv.at[slot, h], base + h, to) for h in range(HEADS)]

    z_even = z % 2 == 0
    near_z = near_send(40, pos, zpart)
    near_x = near_send(44, pos, xpart)
    relay = near_send(48, (pos + 1) % 2, zpart)

    def local_fwd(h):
        for ib in range(2):
            nk = 256 * (ib + 1)
            qs = slice(ib * 256, ib * 256 + 256)
            st = nt(k[0:nk, hc(h)], q[qs, hc(h)]) * SCALE
            jj = iota((nk, 256), 0)
            qq = iota((nk, 256), 1) + ib * 256
            st = jnp.where(jj <= qq, st, NEG)
            mx = jnp.max(st, 0, keepdims=True).astype(BF).astype(F32)
            e = jnp.exp(st - mx)
            el = low(e)
            e_l[h, 0:nk, qs] = el
            o_l[h, :, qs] = tn(v[0:nk, hc(h)], el)
            st_l[h, 0:1, qs] = mx
            st_l[h, 1:2, qs] = jnp.sum(e, 0, keepdims=True)

    local_fwd(0)
    local_fwd(1)
    loads[3].wait()
    pl.semaphore_wait(barrier, len(partners))

    p1 = [rc(p1s.at[yx[n][0]], p1r.at[xh, y], n, dev(yx[n][0], z, yx[n][1])) for n in range(7)]
    for cp in p1:
        cp.start()
    p1r[xh, y] = p1s[y]

    @pl.when(pos != 3)
    def _():
        for cp in near_x:
            cp.start()

    @pl.when(z_even)
    def _():
        for cp in near_z:
            cp.start()

    def pieces(src, dst, base, to, count):
        size = ROWS // count
        return [rc(src.at[pl.ds(size * n, size)], dst.at[pl.ds(size * n, size)], base + n, to)
                for n in range(count)]

    cg_x = pieces(g, gbuf.at[1], 52, across, 4)
    cg_core = rc(g, gbuf.at[0], 28, core)
    cg_f = pieces(gbuf.at[1], gbuf.at[2], 56, core, 4)
    cg_core.start()
    local_fwd(2)
    local_fwd(3)
    for cp in p1:
        cp.wait()
    for hh in range(2):
        got = [p1r[hh, t].astype(F32) for t in range(NY)]
        fkv[z, hh] = low(jnp.concatenate([x[0:8] for x in got] + [x[8:16] for x in got], 0))
    p3 = [rc(fkv.at[z], fkv.at[z], 7 + d, zps[d]) for d in range(7)]
    for d in (3, 2, 4, 1, 5, 0, 6):
        p3[d].start()
    for cp in cg_x:
        cp.start()
    got = [p1r[xh, t].astype(F32) for t in range(NY)]
    fq = low(jnp.concatenate([x[16:24] for x in got] + [jnp.zeros((96, HD), F32)], 0))

    def grad_part(slot, half):
        src = [(l, c), (l, 1 - c), (1 - l, c), (1 - l, 1 - c)][slot]
        cols = pl.ds(pl.multiple_of((src[0] * 2 + src[1]) * ROWS, ROWS), ROWS)
        r = slice(256 * half, 256 * half + 256)
        part = nt(w[:, cols], g[r, :] if slot == 0 else gbuf[slot - 1, r, :])
        if slot:
            part = part + gacc[:, r]
        gacc[:, r] = part

    loads[4].wait()
    for n in range(2):
        grad_part(0, n)
    cg_core.wait()
    for n in range(2):
        grad_part(1, n)

    @pl.when(z_even)
    def _():
        for h in range(HEADS):
            near_x[h].wait_recv()
            relay[h].start()

    def scores(kk, qq, vv, seen):
        st = nt(kk, qq) * SCALE
        st = jnp.where(seen, st, NEG)
        mx = jnp.max(st, 0, keepdims=True).astype(BF).astype(F32)
        e = jnp.exp(st - mx)
        el = low(e)
        hi, lo = hi_lo(jnp.sum(e, 0, keepdims=True))
        return el, low(jnp.concatenate([tn(vv, el), mx, hi, lo, jnp.zeros((13, HD), F32)], 0))

    jn = iota((ROWS, HD), 0)
    an = iota((ROWS, HD), 1)
    near_seen = jn <= pos * 128 + an
    key_index = ((jn // 8) % 4) * 128 + (jn // 64) * 16 + ((jn // 32) % 2) * 8 + jn % 8
    query_index = (an // 8) * 128 + z * 16 + xh * 8 + an % 8
    far_seen = key_index <= query_index

    def near_k(h):
        return nkv[:, h, 0:128, :].reshape(ROWS, HD)

    def near_v(h):
        return nkv[:, h, 128:256, :].reshape(ROWS, HD)

    jt = iota((ROWS, HD), 0)
    at = iota((ROWS, HD), 1)
    for h in range(HEADS):
        back_n[h] = jnp.where(jt == 4 * at + offs[0, h], 1.0, 0.0).astype(BF)
        back_f[h] = jnp.where((jt == 64 * at + offs[1, h]) & (at < 8), 1.0, 0.0).astype(BF)[:, 0:16]

    for cp in p3:
        cp.wait_recv()
    far_k = fkv[:, :, 0:32, :].reshape(ROWS, HD)
    far_v = fkv[:, :, 32:64, :].reshape(ROWS, HD)
    el, block = scores(far_k, fq, far_v, far_seen)
    e_f[...] = el
    fo[y] = block
    p4 = [rc(fo.at[y], fo.at[y], 14 + d, yps[d]) for d in range(3)]
    for cp in p4:
        cp.start()

    for h in range(HEADS):
        @pl.when(z % 2 == 1)
        def _():
            near_z[h].wait_recv()
            relay[h].wait_recv()

        @pl.when(pos == 3)
        def _():
            near_x[h].wait_recv()

        qq = low(nn(a_n[h], q[:, hc(h)]))
        q_n[h] = qq
        el, block = scores(near_k(h), qq, near_v(h), near_seen)
        e_n[h] = el
        o_n[h] = block

    lane = iota((1, ROWS), 1)

    def spread(block, sel):
        both = nn(block, sel)
        return both[0:HD], both[HD:HD + 1], both[HD + 1:HD + 2] + both[HD + 2:HD + 3]

    def picked(cf, inner, sel):
        c_hi, c_lo = hi_lo(cf)
        i_hi, i_lo = hi_lo(inner)
        rows = jnp.concatenate([c_hi, c_lo, i_hi, i_lo, jnp.zeros((12, ROWS), F32)], 0)
        return nt(low(rows), sel)

    def combine(h):
        on, mn, sn = spread(o_n[h], a_n[h])
        of, mf, sf = spread(fo[h], a_f[h])
        mn = jnp.where(lane % 4 == offs[0, h], mn, NEG)
        mf = jnp.where(lane % 64 == offs[1, h], mf, NEG)
        ml = st_l[h, 0:1, :]
        top = jnp.maximum(ml, jnp.maximum(mn, mf))
        wl, wn, wf = jnp.exp(ml - top), jnp.exp(mn - top), jnp.exp(mf - top)
        total = st_l[h, 1:2, :] * wl + sn * wn + sf * wf
        inv = 1.0 / total
        out = low((o_l[h] * wl + on * wn + of * wf) * inv)
        att[hc(h), :] = out
        att_t[:, hc(h)] = out.T
        c_l[h, 0:1, :] = wl * inv
        c_l[h, 1:2, :] = wn * inv
        c_l[h, 2:3, :] = wf * inv

    def row_stats(h):
        inner = jnp.sum(dot_[hc(h), :].astype(F32) * att[hc(h), :].astype(F32), 0, keepdims=True)
        inn[h, 0:1, :] = inner
        far = picked(c_l[h, 2:3, :], inner, a_f[h])
        p5s[h] = low(jnp.concatenate([nn(f16[h], do_[:, hc(h)])[:8], far[:8]], 0))
        c_n[h] = picked(c_l[h, 1:2, :], inner, a_n[h])

    for cp in p4:
        cp.wait()
    for h in range(HEADS):
        combine(h)
    def mixed_part(ll, cc, n):
        cols = pl.ds(pl.multiple_of((ll * 2 + cc) * ROWS, ROWS), ROWS)
        return nn(att_t[256 * n:256 * n + 256, :], w[:, cols])

    def half(n):
        return pl.ds(256 * n, 256)

    cm0 = pieces(mcs.at[0], mcr.at[0], 60, core, 2)
    cm1 = pieces(mcs.at[1], mcr.at[1], 62, core, 2)
    cmx = [rc(mxs.at[pl.ds(64 * n, 64)], mxr.at[pl.ds(64 * n, 64)], 64 + n, across) for n in range(8)]

    def send_mixed(n):
        if n >= 4:
            cmx[n - 4].wait_send()
        cmx[n].start()

    for n in range(2):
        mcs[0, half(n), :] = low(mixed_part(1 - l, 1 - c, n))
        cm0[n].start()
    for n in range(2):
        for i in (2 * n, 2 * n + 1):
            cg_x[i].wait_recv()
            cg_f[i].start()
        grad_part(2, n)
    for n in range(2):
        cg_f[2 * n].wait_recv()
        cg_f[2 * n + 1].wait_recv()
        grad_part(3, n)
        r = slice(256 * n, 256 * n + 256)
        dot_[:, r] = low(gacc[:, r])
        do_[r, :] = dot_[:, r].T
    for h in range(HEADS):
        row_stats(h)
    p5 = [rc(p5s.at[ys[d]], p5r.at[y], 17 + d, yps[d]) for d in range(3)]
    for cp in p5:
        cp.start()
    p5r[y] = p5s[y]

    for n in range(2):
        part = mixed_part(1 - l, c, n)
        cm0[n].wait()
        mxs[half(n), :] = low(part + mcr[0, half(n), :].astype(F32))
        send_mixed(2 * n)
        send_mixed(2 * n + 1)

    def near_bwd(h):
        dd = low(nn(a_n[h], do_[:, hc(h)]))
        prob = e_n[h].astype(F32) * (c_n[h, 0:1, :] + c_n[h, 1:2, :])
        ds = low(prob * (nt(near_v(h), dd) - (c_n[h, 2:3, :] + c_n[h, 3:4, :])))
        ng[:, h, 0:128, :] = low(nn(ds, q_n[h]) * SCALE).reshape(4, HD, HD)
        ng[:, h, 128:256, :] = low(nn(low(prob), dd)).reshape(4, HD, HD)
        dqt[h] = nn(low(tn(near_k(h), ds) * SCALE), a_n[h])

    def back_copy(slot, into, base, to):
        return [rc(ng.at[slot, h], nrb.at[into, h], base + h, to) for h in range(HEADS)]

    back_z = back_copy(0, 0, 72, zpart)
    back_x = back_copy((pos + 3) % 4, 1, 76, xpart)
    back_rx = back_copy(0, 2, 80, xpart)
    back_rz = back_copy(1, 2, 80, zpart)
    for h in range(HEADS):
        near_bwd(h)

        @pl.when(z % 2 == 1)
        def _():
            back_z[h].start()
            back_x[h].start()

    for cp in p5:
        cp.wait()
    got = [p5r[t].astype(F32) for t in range(NY)]
    fd = low(jnp.concatenate([x[0:8] for x in got] + [jnp.zeros((96, HD), F32)], 0))
    stat = got[0][8:16] + got[1][8:16] + got[2][8:16] + got[3][8:16]
    far_k = fkv[:, :, 0:32, :].reshape(ROWS, HD)
    far_v = fkv[:, :, 32:64, :].reshape(ROWS, HD)
    prob = e_f[...].astype(F32) * (stat[0:1] + stat[1:2])
    ds = low(prob * (nt(far_v, fd) - (stat[2:3] + stat[3:4])))
    fgr[:, :, 0:32, :] = low(nn(ds, fq) * SCALE).reshape(NZ, 2, 32, HD)
    fgr[:, :, 32:64, :] = low(nn(low(prob), fd)).reshape(NZ, 2, 32, HD)
    p6 = [rc(fgr.at[(z + d + 1) % NZ], rz.at[d], 20 + d, zps[d]) for d in range(7)]
    for d in (3, 2, 4, 1, 5, 0, 6):
        p6[d].start()
    fdq = tn(ds, far_k)[0:32] * SCALE

    def local_bwd(h):
        for ib in range(2):
            nk = 256 * (ib + 1)
            qs = slice(ib * 256, ib * 256 + 256)
            prob = e_l[h, 0:nk, qs].astype(F32) * c_l[h, 0:1, qs]
            dp = nn(v[0:nk, hc(h)], dot_[hc(h), qs])
            ds = low(prob * (dp - inn[h, 0:1, qs]))
            vt = nn(low(prob), do_[qs, hc(h)])
            kt = nn(ds, q[qs, hc(h)]) * SCALE
            if ib == 0:
                dva[0:nk, hc(h)] = vt
                dka[0:nk, hc(h)] = kt
            else:
                dva[0:256, hc(h)] = dva[0:256, hc(h)] + vt[0:256]
                dka[0:256, hc(h)] = dka[0:256, hc(h)] + kt[0:256]
                dva[256:512, hc(h)] = vt[256:512]
                dka[256:512, hc(h)] = kt[256:512]
            qt = tn(k[0:nk, hc(h)], ds) * SCALE + dqt[h, :, qs]
            dqa[qs, hc(h)] = qt.T

    def add_block(dst, src):
        dst[...] = low(dst[...].astype(F32) + src[...].astype(F32))

    def relay_back(heads):
        @pl.when(pos == 1)
        def _():
            for h in heads:
                back_z[h].wait_recv()
                add_block(ng.at[0, h], nrb.at[0, h])
                back_rx[h].start()

        @pl.when(pos == 3)
        def _():
            for h in heads:
                back_x[h].wait_recv()
                add_block(ng.at[1, h], nrb.at[1, h])
                back_rz[h].start()

    relay_back((0, 1))
    local_bwd(0)
    relay_back((2, 3))
    send_mixed(4)
    local_bwd(1)
    send_mixed(5)
    local_bwd(2)
    for cp in p6:
        cp.wait_recv()
    total = fgr[z].astype(F32)
    for d in range(7):
        total = total + rz[d].astype(F32)
    fgr[z] = low(total)
    for hh in range(2):
        for t in range(NY):
            r = slice(8 * t, 8 * t + 8)
            third = jnp.where(xh == hh, fdq[r], 0.0)
            p8s[hh, t] = low(jnp.concatenate(
                [total[hh, r], total[hh, 32 + 8 * t:40 + 8 * t], third, pad8], 0))
    p8 = [rc(p8s.at[yx[n][1], yx[n][0]], p8r.at[xh, y], 29 + n, dev(yx[n][0], z, yx[n][1])) for n in range(7)]
    for cp in p8:
        cp.start()
    p8r[xh, y] = p8s[xh, y]

    local_bwd(3)
    send_mixed(6)
    for n in range(2):
        mcs[1, half(n), :] = low(mixed_part(l, 1 - c, n))
        cm1[n].start()
    send_mixed(7)
    for n in range(2):
        mkeep[half(n), :] = mixed_part(l, c, n)

    for n in range(4, 8):
        cmx[n].wait_send()
    for n in range(2):
        cm1[n].wait()
        for i in range(4):
            cmx[4 * n + i].wait_recv()
        mixed[half(n), :] = low(mkeep[half(n), :] + mcr[1, half(n), :].astype(F32) + mxr[half(n), :].astype(F32))

    out_mixed = pltpu.make_async_copy(mixed, mixed_h, outs.at[0])
    out_mixed.start()

    def take(copies, slot, into):
        for cp in copies:
            cp.wait_recv()
        add_block(ng.at[slot], nrb.at[into])

    @pl.when(pos == 0)
    def _():
        take(back_z, 0, 0)
        take(back_rx, 0, 2)

    @pl.when(pos == 1)
    def _():
        take(back_rz, 1, 2)

    @pl.when(pos == 2)
    def _():
        take(back_x, 2, 1)

    for cp in p8:
        cp.wait()
    out_rest = []
    for h in range(HEADS):
        x = p8r[0, h].astype(F32) + p8r[1, h].astype(F32)
        wide = jnp.concatenate([x[0:8], x[8:16], x[16:24]], 1)
        far = nn(back_f[h], low(jnp.concatenate([wide, jnp.zeros((8, 3 * HD), F32)], 0)))
        dk[:, hc(h)] = low(dka[:, hc(h)] + nn(back_n[h], ng[pos, h, 0:128, :]) + far[:, 0:HD])
        dv[:, hc(h)] = low(dva[:, hc(h)] + nn(back_n[h], ng[pos, h, 128:256, :]) + far[:, HD:2 * HD])
        dq[:, hc(h)] = low(dqa[:, hc(h)] + far[:, 2 * HD:])
        for n, (a, b) in enumerate([(dk, dk_h), (dv, dv_h), (dq, dq_h)]):
            cp = pltpu.make_async_copy(a.at[:, hc(h)], b.at[:, hc(h)], outs.at[1 + 3 * h + n])
            cp.start()
            out_rest.append(cp)

    for cp in p3 + p6 + cg_x + cg_f:
        cp.wait_send()

    @pl.when(pos != 3)
    def _():
        for cp in near_x:
            cp.wait_send()

    @pl.when(z_even)
    def _():
        for cp in near_z + relay:
            cp.wait_send()

    @pl.when(pos == 1)
    def _():
        for cp in back_rx:
            cp.wait_send()

    @pl.when(pos == 3)
    def _():
        for cp in back_rz:
            cp.wait_send()

    @pl.when(z % 2 == 1)
    def _():
        for cp in back_x + back_z:
            cp.wait_send()
    for cp in [out_mixed] + out_rest:
        cp.wait()


def hand_on(a, b, c, d, a2, b2, c2, d2, hold, in_sem, out_sem):
    pairs = [(x, x2, j, pl.ds(256 * n, 256)) for j, (x, x2) in enumerate([(a, a2), (b, b2), (c, c2), (d, d2)])
             for n in range(2)]
    ins = [pltpu.make_async_copy(x.at[r], hold.at[j, r], in_sem.at[i]) for i, (x, _, j, r) in enumerate(pairs)]
    outs = [pltpu.make_async_copy(hold.at[j, r], x, out_sem.at[i])
            for i, (x, j, r) in enumerate([(x2.at[r], j, r) for _, x2, j, r in pairs])]
    for cp in ins:
        cp.start()
    for i, o in zip(ins, outs):
        i.wait()
        o.start()
    for cp in outs:
        cp.wait()


def local(queries, key_rows, value_rows, out_weight, grad_out, offsets):
    hbm = pl.BlockSpec(memory_space=pl.ANY)
    shape = jax.ShapeDtypeStruct((ROWS, ROWS), BF)
    V = pltpu.VMEM
    dma = pltpu.SemaphoreType.DMA
    wide = (ROWS, ROWS)
    outs = pl.pallas_call(
        kernel,
        out_shape=(shape,) * 4,
        in_specs=[pl.BlockSpec(memory_space=pltpu.SMEM)] + [hbm] * 5,
        out_specs=(hbm,) * 4,
        scratch_shapes=[
            V(wide, BF), V(wide, BF), V(wide, BF), V(wide, BF),
            V(wide, BF), V(wide, BF), V(wide, BF), V((ROWS, 4 * ROWS), BF), V(wide, BF),
            V((3, ROWS, ROWS), BF), V(wide, F32), V(wide, BF), V(wide, BF),
            V((4, HEADS, 256, HD), BF),
            V((HEADS, ROWS, ROWS), BF), V((HEADS, ROWS, HD), BF), V((ROWS, HD), BF),
            V((HEADS, HD, ROWS), F32), V((HEADS, 144, HD), BF),
            V((HEADS, 8, ROWS), F32), V((HEADS, 8, HD), F32),
            V((HEADS, HD, HD), BF),
            V((HEADS, HD, ROWS), BF), V((HEADS, HD, ROWS), BF), V((HEADS, 16, ROWS), BF),
            V(wide, BF),
            V((HEADS, 8, ROWS), F32), V((HEADS, 16, HD), F32), V((HEADS, 8, ROWS), F32),
            V((HEADS, HD, ROWS), F32), V(wide, F32), V(wide, F32), V(wide, F32),
            V((NY, 32, HD), BF), V((2, NY, 32, HD), BF), V((NZ, 2, 64, HD), BF), V((NY, 144, HD), BF),
            V((NY, 16, HD), BF), V((NY, 16, HD), BF), V((NZ, 2, 64, HD), BF), V((NZ - 1, 2, 64, HD), BF),
            V((2, NY, 32, HD), BF), V((2, NY, 32, HD), BF),
            V((4, HEADS, 256, HD), BF), V((3, HEADS, 256, HD), BF),
            V((2, ROWS, ROWS), BF), V((2, ROWS, ROWS), BF), V(wide, F32),
            V(wide, BF), V(wide, BF),
            V((HEADS, ROWS, HD), BF), V((HEADS, ROWS, 16), BF), V(wide, BF),
            dma((5,)), dma((13,)), dma((84,)), dma((84,)),
        ],
        compiler_params=pltpu.CompilerParams(
            collective_id=0, has_side_effects=True, vmem_limit_bytes=56 << 20),
        cost_estimate=pl.CostEstimate(flops=4_400_000_000, bytes_accessed=8 << 20, transcendentals=1_400_000),
        name="dilated",
    )(offsets, queries, key_rows, value_rows, out_weight, grad_out)
    return pl.pallas_call(
        hand_on,
        out_shape=(shape,) * 4,
        in_specs=[hbm] * 4,
        out_specs=(hbm,) * 4,
        scratch_shapes=[V((4, ROWS, ROWS), BF), dma((8,)), dma((8,))],
        name="hand_on",
    )(*outs)


def solution(mesh):
    return jax.shard_map(
        local,
        mesh=mesh,
        in_specs=(
            P("seq", "mp"),
            P("seq", "mp"),
            P("seq", "mp"),
            P("mp", None),
            P("seq", "mp"),
            P(None, "mp"),
        ),
        out_specs=(P("seq", "mp"), P("seq", "mp"), P("seq", "mp"), P("seq", "mp")),
        check_vma=False,
    )
```
